32 devices in a mesh: task: 4 (over y, x), dp: 8 (over z, core).
Axes of the slice: x: 2, y: 2, z: 4, core: 2. Of those that a mesh axis runs over, the one named last changes fastest.
Arguments:
- images: bfloat16 [144, 96, 512], P('dp'), may hold values from -6 to 6
- conv_first: float32 [3, 3, 512, 512], P(None, None, None, 'dp'), may hold values from -0.09375 to 0.09375
- conv_second: float32 [3, 3, 512, 512], P(None, None, None, 'dp'), may hold values from -0.09375 to 0.09375
- conv_third: float32 [3, 3, 512, 512], P(None, None, None, 'dp'), may hold values from -0.09375 to 0.09375
- trunk_gains: float32 [3, 512], replicated, may hold values from 0.1 to 1.9
- trunk_biases: float32 [3, 512], replicated, may hold values from -3 to 3
- attend_in: float32 [3, 512, 512], P(None, None, 'dp'), may hold values from -0.25 to 0.25
- attend_mask: float32 [3, 512, 512], P(None, None, 'dp'), may hold values from -0.25 to 0.25
- attend_out: float32 [3, 3, 3, 512, 512], P(None, None, None, None, 'dp'), may hold values from -0.09375 to 0.09375
- branch_gains: float32 [3, 3, 512], replicated, may hold values from 0.1 to 1.9
- branch_biases: float32 [3, 3, 512], replicated, may hold values from -3 to 3
- size_class: int32 [8], replicated, may hold values from 0 to 1, as said below
- domain_tags: int32 [8, 4], replicated, may hold values 0 or 1
- trunk_cotangent: bfloat16 [72, 48, 512], P('dp'), may hold values from -6 to 6
- task_cotangent: bfloat16 [3, 72, 48, 512], P(None, 'dp'), may hold values from -6 to 6
Outputs:
- trunk_features: bfloat16 [72, 48, 512], P('dp')
- task_features: bfloat16 [3, 72, 48, 512], P(None, 'dp')
- images_grad: float32 [144, 96, 512], P('dp')
- conv_first_grad: float32 [3, 3, 512, 512], P(None, None, None, 'dp')
- conv_second_grad: float32 [3, 3, 512, 512], P(None, None, None, 'dp')
- conv_third_grad: float32 [3, 3, 512, 512], P(None, None, None, 'dp')
- trunk_gains_grad: float32 [3, 512], replicated
- trunk_biases_grad: float32 [3, 512], replicated
- attend_in_grad: float32 [3, 512, 512], P(None, None, 'dp')
- attend_mask_grad: float32 [3, 512, 512], P(None, None, 'dp')
- attend_out_grad: float32 [3, 3, 3, 512, 512], P(None, None, None, None, 'dp')
- branch_gains_grad: float32 [3, 3, 512], replicated
- branch_biases_grad: float32 [3, 3, 512], replicated
The draws below stay inside these ranges and needn't reach their ends.
Inputs may be any that keep to these rules, and one draw needn't show every extreme that they name: Of the slots 2k and 2k + 1 exactly one has size_class 0.
All inputs are finite; a program needn't handle non-finite values.
Results may differ from the reference program's by a relative error of at most 0.025.
Values may be sent and summed in bfloat16 or wider, within the bound.
No kernel may reach another device: no remote copies, remote signals or barrier semaphores. Data moves between devices by JAX's collectives and lax.ppermute only.
A program may use at most 192 MiB of HBM per device.

```python
import jax
import jax.numpy as jnp
from jax import lax

CHANNELS = 512
HEIGHT = 36
WIDTH = 48
BAND = 18
HALF_WIDTH = 24
CANVAS = 2
TASKS = 3
SLOTS = 8
ROWS = 144
COLS = 96


def draw_size_class(key, part):
    key = jax.random.fold_in(key, 11)
    pair_count = SLOTS // 2
    large_at = jax.random.randint(key, (pair_count,), 0, 2)
    classes = 1 - (jnp.arange(2)[None, :] == large_at[:, None]).astype(jnp.int32)
    return classes.reshape(SLOTS).astype(jnp.int32)


def with_ends(values, own_key, smallest, largest):
    dims = values.shape
    spot = [jax.random.randint(jax.random.fold_in(own_key, axis), (), 0, dims[axis]) for axis in range(len(dims))]
    values = values.at[tuple(spot)].set(smallest)
    longest = dims.index(max(dims))
    spot[longest] = (spot[longest] + 1) % dims[longest]
    return values.at[tuple(spot)].set(largest)


def levels(key, extent, split, low, top_value):
    def one(dim, parts):
        draws = jax.random.uniform(jax.random.fold_in(jax.random.fold_in(key, 6), dim), (parts,), jnp.float32, low / len(split), top_value / len(split))
        return jnp.repeat(jnp.exp(draws), extent[dim] // parts).reshape((-1,) + (1,) * (len(extent) - dim - 1))

    level = one(*split[0])
    for cut in split[1:]:
        level = level * one(*cut)
    return level


def gaussian(rng, extent, deviation, limit, shards=(), dtype=jnp.bfloat16):
    loudness = levels(rng, extent, shards, -0.22, 0.18) if shards else 1.0
    drawn = jax.random.normal(rng, extent, jnp.float32) * deviation * loudness
    return jnp.minimum(jnp.maximum(drawn, -limit), limit).astype(dtype)


def setup_inputs(seed: int = 0) -> dict:
    keys = jax.random.split(jax.random.key(seed), 16)
    images = gaussian(keys[0], (ROWS, COLS, CHANNELS), 1.0, 6.0, ((0, 8),))
    conv_first = gaussian(keys[1], (3, 3, CHANNELS, CHANNELS), (9 * CHANNELS) ** -0.5, 0.09375, ((3, 8),), jnp.float32)
    conv_second = gaussian(keys[2], (3, 3, CHANNELS, CHANNELS), (9 * CHANNELS) ** -0.5, 0.09375, ((3, 8),), jnp.float32)
    conv_third = gaussian(keys[3], (3, 3, CHANNELS, CHANNELS), (9 * CHANNELS) ** -0.5, 0.09375, ((3, 8),), jnp.float32)
    trunk_gains = jnp.clip(1.0 + 0.18 * jax.random.normal(keys[4], (3, CHANNELS), jnp.float32), 0.1, 1.9)
    trunk_biases = gaussian(keys[5], (3, CHANNELS), 0.5, 3.0, (), jnp.float32)
    attend_in = gaussian(keys[6], (TASKS, CHANNELS, CHANNELS), CHANNELS ** -0.5, 0.25, ((2, 8),), jnp.float32)
    attend_mask = gaussian(keys[7], (TASKS, CHANNELS, CHANNELS), CHANNELS ** -0.5, 0.25, ((2, 8),), jnp.float32)
    attend_out = gaussian(keys[8], (TASKS, 3, 3, CHANNELS, CHANNELS), (9 * CHANNELS) ** -0.5, 0.09375, ((4, 8),), jnp.float32)
    branch_gains = jnp.clip(1.0 + 0.18 * jax.random.normal(keys[9], (TASKS, 3, CHANNELS), jnp.float32), 0.1, 1.9)
    branch_biases = gaussian(keys[10], (TASKS, 3, CHANNELS), 0.5, 3.0, (), jnp.float32)
    size_class = draw_size_class(jax.random.fold_in(keys[15], 71), 0)
    domain_tags = with_ends((jax.random.randint(keys[12], (SLOTS, 4), 0, 4) < 1).astype(jnp.int32), jax.random.fold_in(keys[12], 1), 0, 1)
    trunk_cotangent = gaussian(keys[13], (ROWS // 2, COLS // 2, CHANNELS), 1.0, 6.0, ((0, 8),))
    task_cotangent = gaussian(keys[14], (TASKS, ROWS // 2, COLS // 2, CHANNELS), 1.0, 6.0, ((1, 8),))
    return dict(images=images, conv_first=conv_first, conv_second=conv_second, conv_third=conv_third, trunk_gains=trunk_gains, trunk_biases=trunk_biases, attend_in=attend_in, attend_mask=attend_mask, attend_out=attend_out, branch_gains=branch_gains, branch_biases=branch_biases, size_class=size_class, domain_tags=domain_tags, trunk_cotangent=trunk_cotangent, task_cotangent=task_cotangent)


EPSILON = 1e-05
OFFSETS = ((-1, -1), (-1, 0), (-1, 1), (0, -1), (0, 0), (0, 1), (1, -1), (1, 0), (1, 1))

@jax.custom_vjp
def low(v):
    return lax.optimization_barrier(v.astype(jnp.bfloat16)).astype(jnp.float32)

@jax.custom_vjp
def low_back(v):
    return v

def low_keep(v):
    return (low(v), None)

def low_pass(kept, grad):
    return (grad,)

def back_keep(v):
    return (v, None)

def back_low(kept, grad):
    return (low(grad),)
low.defvjp(low_keep, low_pass)
low_back.defvjp(back_keep, back_low)

def domain_counts(size_class, domain_tags):
    big_area = HEIGHT * WIDTH
    small_area = BAND * HALF_WIDTH
    ones_count = jnp.sum(jnp.where(size_class == 0, big_area * domain_tags[:, 0], small_area * lax.optimization_barrier(jnp.sum(domain_tags, axis=1))))
    all_count = size_class.shape[0] * big_area
    return jnp.maximum(jnp.stack([all_count - ones_count, ones_count]).astype(jnp.float32), 1.0)

def build_masks(up_valid, down_valid, left_valid, right_valid, mask_type):
    result_list = []
    for row_step, col_step in OFFSETS:
        current = jnp.ones(up_valid.shape, jnp.bool_)
        if row_step == -1:
            current = current & up_valid
        if row_step == 1:
            current = current & down_valid
        if col_step == -1:
            current = current & left_valid
        if col_step == 1:
            current = current & right_valid
        result_list.append(current.astype(mask_type)[:, :, None])
    return result_list

def layout(size_class, domain_tags):
    row_number = jnp.arange(ROWS)
    column = jnp.arange(COLS)
    pair_index = row_number // HEIGHT
    bottom_half = row_number % HEIGHT // BAND
    band_row = row_number % BAND
    canvas_of = column // WIDTH
    in_canvas = column % WIDTH
    slot_index = (pair_index[:, None] * CANVAS + canvas_of[None, :]).astype(jnp.int32)
    small_class = size_class[slot_index] == 1
    slot_tags = domain_tags[slot_index]
    quarter = (bottom_half[:, None] * 2 + (in_canvas >= HALF_WIDTH)[None, :].astype(jnp.int32)).astype(jnp.int32)
    small_tag = jnp.take_along_axis(slot_tags, quarter[:, :, None], axis=2)[:, :, 0]
    domain = jnp.where(small_class, small_tag, slot_tags[:, :, 0]).astype(jnp.float32)[:, :, None]
    up_valid = jnp.logical_not((band_row == 0)[:, None] & (small_class | (bottom_half == 0)[:, None]))
    down_valid = jnp.logical_not((band_row == BAND - 1)[:, None] & (small_class | (bottom_half == 1)[:, None]))
    left_valid = (in_canvas > 0)[None, :] & jnp.logical_not(small_class & (in_canvas == HALF_WIDTH)[None, :])
    right_valid = (in_canvas < WIDTH - 1)[None, :] & jnp.logical_not(small_class & (in_canvas == HALF_WIDTH - 1)[None, :])
    tap_masks = build_masks(up_valid, down_valid, left_valid, right_valid, jnp.float32)
    return (tap_masks, domain, domain_counts(size_class, domain_tags))

def conv_apply(source, kernel, tap_masks):
    row_count, col_count = (source.shape[0], source.shape[1])
    padded = jnp.pad(source, ((1, 1), (1, 1), (0, 0)))
    summed = jnp.zeros((row_count, col_count, kernel.shape[3]), jnp.float32)
    for tap_index, (row_step, col_step) in enumerate(OFFSETS):
        shifted = padded[1 + row_step:1 + row_step + row_count, 1 + col_step:1 + col_step + col_count] * tap_masks[tap_index]
        summed = summed + jnp.einsum('rwc,cd->rwd', shifted, kernel[1 + row_step, 1 + col_step], precision=lax.Precision.HIGHEST)
    return summed

def batch_norm(values, domain, counts, gain, bias):
    other = 1.0 - domain
    squares = values * values
    sums = jnp.stack([lax.optimization_barrier(jnp.sum(values * other, axis=(0, 1))), lax.optimization_barrier(jnp.sum(values * domain, axis=(0, 1)))])
    square_sums = jnp.stack([lax.optimization_barrier(jnp.sum(squares * other, axis=(0, 1))), lax.optimization_barrier(jnp.sum(squares * domain, axis=(0, 1)))])
    means = sums / counts[:, None]
    variance = square_sums / counts[:, None] - means * means
    scales = lax.rsqrt(variance + EPSILON)
    mean_pixel = domain * means[1] + other * means[0]
    scale_pixel = domain * scales[1] + other * scales[0]
    return (values - mean_pixel) * scale_pixel * gain + bias

def pool_mean(values):
    row_count, col_count, channels = values.shape
    return lax.optimization_barrier(jnp.mean(values.reshape(row_count // 2, 2, col_count // 2, 2, channels), axis=(1, 3)))

def reference(images, conv_first, conv_second, conv_third, trunk_gains, trunk_biases, attend_in, attend_mask, attend_out, branch_gains, branch_biases, size_class, domain_tags, trunk_cotangent, task_cotangent):
    tap_masks, domain, counts = layout(size_class, domain_tags)

    def forward(image_values, first_kernel, second_kernel, third_kernel, t_gains, t_biases, in_kernels, mask_kernels, out_kernels, b_gains, b_biases):
        activation = image_values
        kernels = (first_kernel, second_kernel, third_kernel)
        for layer_index in range(3):
            summed = low_back(conv_apply(low(activation), low(kernels[layer_index]), tap_masks))
            activation = jax.nn.silu(batch_norm(summed, domain, counts, t_gains[layer_index], t_biases[layer_index]))
        trunk_out = pool_mean(activation)
        low_shared = low(activation)
        task_list = []
        for task in range(TASKS):
            first_sum = low_back(jnp.einsum('rwc,cd->rwd', low_shared, low(in_kernels[task]), precision=lax.Precision.HIGHEST))
            first_act = jax.nn.silu(batch_norm(first_sum, domain, counts, b_gains[task, 0], b_biases[task, 0]))
            mask_sum = low_back(jnp.einsum('rwc,cd->rwd', low(first_act), low(mask_kernels[task]), precision=lax.Precision.HIGHEST))
            gate_value = jax.nn.sigmoid(batch_norm(mask_sum, domain, counts, b_gains[task, 1], b_biases[task, 1]))
            masked = low_shared * gate_value
            last_sum = low_back(conv_apply(low(masked), low(out_kernels[task]), tap_masks))
            branch_act = jax.nn.silu(batch_norm(last_sum, domain, counts, b_gains[task, 2], b_biases[task, 2]))
            task_list.append(pool_mean(branch_act))
        return (trunk_out, jnp.stack(task_list))
    primals = (images.astype(jnp.float32), conv_first, conv_second, conv_third, trunk_gains, trunk_biases, attend_in, attend_mask, attend_out, branch_gains, branch_biases)
    outputs, pullback = jax.vjp(forward, *primals)
    grads = pullback((trunk_cotangent.astype(jnp.float32), task_cotangent.astype(jnp.float32)))
    return (outputs[0].astype(jnp.bfloat16), outputs[1].astype(jnp.bfloat16), grads[0], grads[1], grads[2], grads[3], grads[4], grads[5], grads[6], grads[7], grads[8], grads[9], grads[10])
```

```python
import functools

import jax
import jax.numpy as jnp
from jax import lax
from jax.experimental import pallas as pl
from jax.experimental.pallas import tpu as pltpu
from jax.sharding import PartitionSpec as P

HEIGHT = 36
WIDTH = 48
BAND = 18
HALF_WIDTH = 24
CANVAS = 2
TASKS = 3
COLS = CANVAS * WIDTH
GROUPS = COLS // HALF_WIDTH
EPSILON = 1e-05
TAPS = 9
TILE_ROWS = 6
MIB = 2**20
BF = jnp.bfloat16
F32 = jnp.float32
NT = (((1,), (1,)), ((), ()))
TN = (((0,), (0,)), ((), ()))

VMEM = pl.BlockSpec(memory_space=pltpu.VMEM)
SMEM = pl.BlockSpec(memory_space=pltpu.SMEM)


def affine(row, co, scale, shift):
    step = row.shape[0] // GROUPS
    return jnp.concatenate(
        [
            row[step * j : step * (j + 1)] * co[4 * scale + j : 4 * scale + j + 1, :]
            + co[4 * shift + j : 4 * shift + j + 1, :]
            for j in range(GROUPS)
        ],
        axis=0,
    )


def scaled(row, co, scale):
    step = row.shape[0] // GROUPS
    return jnp.concatenate(
        [
            row[step * j : step * (j + 1)] * co[4 * scale + j : 4 * scale + j + 1, :]
            for j in range(GROUPS)
        ],
        axis=0,
    )


def sigmoid(v):
    return 0.5 * jnp.tanh(0.5 * v) + 0.5


def silu(v):
    return v * sigmoid(v)


def silu_slope(v):
    s = sigmoid(v)
    return s * (1.0 + v * (1.0 - s))


def norm_coefs(co, base, stats, gain, bias, cnt, info):
    means, scales = [], []
    for d in range(2):
        mean = stats[d : d + 1, :] / cnt[d]
        var = stats[2 + d : 3 + d, :] / cnt[d] - mean * mean
        means.append(mean)
        scales.append(lax.rsqrt(var + EPSILON))
    for j in range(GROUPS):
        one = info[j] == 1
        mean = jnp.where(one, means[1], means[0])
        scale = jnp.where(one, scales[1], scales[0])
        full = scale * gain[...]
        co[4 * base + j : 4 * base + j + 1, :] = full
        co[4 * base + 4 + j : 4 * base + 5 + j, :] = bias[...] - mean * full
        co[4 * base + 8 + j : 4 * base + 9 + j, :] = scale
        co[4 * base + 12 + j : 4 * base + 13 + j, :] = -mean * scale


def grad_coefs(co, base, norm, sums, cnt, info):
    for j in range(GROUPS):
        one = info[j] == 1
        count = jnp.where(one, cnt[1], cnt[0])
        plain = jnp.where(one, sums[1:2, :], sums[0:1, :]) / count
        cross = jnp.where(one, sums[3:4, :], sums[2:3, :]) / count
        full = co[4 * norm + j : 4 * norm + j + 1, :]
        scale = co[4 * norm + 8 + j : 4 * norm + 9 + j, :]
        shift = co[4 * norm + 12 + j : 4 * norm + 13 + j, :]
        co[4 * base + j : 4 * base + j + 1, :] = -full * cross * scale
        co[4 * base + 4 + j : 4 * base + 5 + j, :] = -full * (plain + cross * shift)


def grad_row(g, z, co, norm, base):
    return scaled(g, co, norm) + affine(z, co, base, base + 1)


def add_sums(acc, slot, values):
    step = HALF_WIDTH // 8
    count = values.shape[0] // COLS
    channels = values.shape[1]
    acc[slot] += jnp.sum(
        values.reshape(count, GROUPS, step, 8, channels), axis=(0, 2)
    )


def put_sums(acc, info, out, start):
    for slot in range(2):
        groups = [jnp.sum(acc[slot, j], axis=0, keepdims=True) for j in range(GROUPS)]
        for d in range(2):
            total = jnp.zeros_like(groups[0])
            for j in range(GROUPS):
                total = total + jnp.where(info[j] == d, groups[j], 0.0)
            row = start + 2 * slot + d
            out[row : row + 1, :] = total
    out[start + 4 : start + 8, :] = jnp.zeros((4, out.shape[1]), F32)


def put_edge(out, ref, info, rows):
    start = jnp.where(info[6] == 1, 0, (rows - 1) * COLS)
    out[0:COLS, :] = ref[pl.ds(pl.multiple_of(start, 8), COLS), :].astype(out.dtype)


def make_masks(mk, info):
    col = lax.broadcasted_iota(jnp.int32, mk.shape[1:], 0)
    small = (info[4] == 1, info[5] == 1)
    left = (col == 0) | (col == WIDTH)
    right = (col == WIDTH - 1) | (col == COLS - 1)
    for s in range(2):
        left = left | ((col == s * WIDTH + HALF_WIDTH) & small[s])
        right = right | ((col == s * WIDTH + HALF_WIDTH - 1) & small[s])
    mk[0] = jnp.where(left, 0.0, 1.0)
    mk[1] = jnp.where(right, 0.0, 1.0)


def put_row(taps, at, row, mk):
    parts = row.shape[1] // mk.shape[2]
    left = jnp.concatenate([mk[0]] * parts, axis=1)
    right = jnp.concatenate([mk[1]] * parts, axis=1)
    here = pl.ds(pl.multiple_of(at * COLS, COLS), COLS)
    taps[0, here, :] = (pltpu.roll(row, 1, 0) * left).astype(BF)
    taps[1, here, :] = row.astype(BF)
    taps[2, here, :] = (pltpu.roll(row, COLS - 1, 0) * right).astype(BF)


def put_halo(taps, row, mk, info, rows):
    step = COLS // GROUPS
    keep = [jnp.where(info[4 + j // 2] == 1, 0.0, 1.0) for j in range(GROUPS)]
    row = jnp.concatenate(
        [row[step * j : step * (j + 1)] * keep[j] for j in range(GROUPS)], axis=0
    )
    put_row(taps, jnp.where(info[6] == 1, 0, rows + 1), row, mk)
    put_row(taps, jnp.where(info[6] == 1, rows + 1, 0), jnp.zeros_like(row), mk)


def conv_tile(taps, w, at, rows, transpose):
    acc = None
    channels = taps.shape[2]
    for t in range(TAPS):
        di, dj = divmod(t, 3)
        a = taps[dj, pl.ds(pl.multiple_of((at + di) * COLS, COLS), rows * COLS), :]
        if transpose:
            k = w[:, (8 - t) * channels : (9 - t) * channels]
            r = jnp.dot(a, k, preferred_element_type=F32)
        else:
            k = w[:, t * channels : (t + 1) * channels]
            r = lax.dot_general(a, k, NT, preferred_element_type=F32)
        acc = r if acc is None else acc + r
    return acc


def row_at(r):
    return pl.ds(pl.multiple_of(r * COLS, COLS), COLS)


def tile_at(m, rows):
    return pl.ds(pl.multiple_of(m * rows * COLS, COLS), rows * COLS)


def loop(count, body):
    def step(i, carry):
        body(i)
        return carry

    lax.fori_loop(0, count, step, 0)


def pooled(buf, values):
    half = COLS // 2
    parts, _, lanes = buf.shape
    out = []
    for c in range(parts):
        buf[c] = values[:, c * lanes : (c + 1) * lanes]
        out.append(buf[c, pl.ds(0, half, stride=2), :] + buf[c, pl.ds(1, half, stride=2), :])
    return jnp.concatenate(out, axis=1) * 0.25


def spread(buf, values):
    half = COLS // 2
    parts, _, lanes = buf.shape
    quarter = values.astype(F32) * 0.25
    out = []
    for c in range(parts):
        part = quarter[:, c * lanes : (c + 1) * lanes]
        buf[c, pl.ds(0, half, stride=2), :] = part
        buf[c, pl.ds(1, half, stride=2), :] = part
        out.append(buf[c])
    return jnp.concatenate(out, axis=1)


def first_conv_kernel(rows, info, x, halo, w, z, pay, quarter, taps, mk, acc):
    make_masks(mk, info)
    acc[...] = jnp.zeros_like(acc)
    loop(rows, lambda r: put_row(taps, r + 1, x[row_at(r), :].astype(F32), mk))
    put_halo(taps, halo[...].astype(F32), mk, info, rows)
    conv_finish(rows, info, w, z, pay, quarter, taps, acc)


def conv_finish(rows, info, w, z, pay, quarter, taps, acc):
    def tile(m):
        out = conv_tile(taps, w, m * TILE_ROWS, TILE_ROWS, False)
        z[tile_at(m, TILE_ROWS), :] = out
        add_sums(acc, 0, out)
        add_sums(acc, 1, out * out)

    loop(rows // TILE_ROWS, tile)
    if quarter is not None:
        width = quarter.shape[2]
        quarter[...] = taps[:, :, pl.ds(pl.multiple_of(info[7] * width, width), width)]
    put_edge(pay, z, info, rows)
    put_sums(acc, info, pay, COLS)


def conv_kernel(
    rows, info, cnt, x, recv, stats, gain, bias, w, z, pay, quarter, taps, mk, acc, co
):
    make_masks(mk, info)
    acc[...] = jnp.zeros_like(acc)
    norm_coefs(co, 0, stats, gain, bias, cnt, info)
    loop(rows, lambda r: put_row(taps, r + 1, silu(affine(x[row_at(r), :], co, 0, 1)), mk))
    put_halo(taps, silu(affine(recv[0:COLS, :], co, 0, 1)), mk, info, rows)
    conv_finish(rows, info, w, z, pay, quarter, taps, acc)


def enter_kernel(
    rows, info, cnt, x, recv, stats, gain, bias, w, low, pool, u, pay, acc, co, buf
):
    acc[...] = jnp.zeros_like(acc)
    norm_coefs(co, 0, stats, gain, bias, cnt, info)

    def pair(i):
        first = silu(affine(x[row_at(2 * i), :], co, 0, 1))
        second = silu(affine(x[row_at(2 * i + 1), :], co, 0, 1))
        low[row_at(2 * i), :] = first.astype(BF)
        low[row_at(2 * i + 1), :] = second.astype(BF)
        half = COLS // 2
        pool[pl.ds(pl.multiple_of(i * half, half), half), :] = pooled(
            buf, first + second
        ).astype(BF)

    loop(rows // 2, pair)
    low[rows * COLS : (rows + 1) * COLS, :] = silu(
        affine(recv[0:COLS, :], co, 0, 1)
    ).astype(BF)

    def tile(m):
        here = tile_at(m, TILE_ROWS)
        out = lax.dot_general(low[here, :], w[...], NT, preferred_element_type=F32)
        u[here, :] = out
        add_sums(acc, 0, out)
        add_sums(acc, 1, out * out)

    loop(rows // TILE_ROWS, tile)
    put_sums(acc, info, pay, 0)


def mask_kernel(rows, info, cnt, u, stats, gain, bias, w, p, q, pay, acc, co):
    acc[...] = jnp.zeros_like(acc)
    norm_coefs(co, 0, stats, gain, bias, cnt, info)

    def each(r):
        p[row_at(r), :] = silu(affine(u[row_at(r), :], co, 0, 1)).astype(BF)

    loop(rows, each)

    def tile(m):
        here = tile_at(m, TILE_ROWS)
        out = lax.dot_general(p[here, :], w[...], NT, preferred_element_type=F32)
        q[here, :] = out
        add_sums(acc, 0, out)
        add_sums(acc, 1, out * out)

    loop(rows // TILE_ROWS, tile)
    put_edge(pay, q, info, rows)
    put_sums(acc, info, pay, COLS)


def branch_conv_kernel(
    rows, info, cnt, low, q, recv, stats, gain, bias, w, y, pay, taps, mk, acc, co
):
    make_masks(mk, info)
    acc[...] = jnp.zeros_like(acc)
    norm_coefs(co, 0, stats, gain, bias, cnt, info)

    def masked(source, gated):
        return source.astype(F32) * sigmoid(affine(gated, co, 0, 1))

    loop(rows, lambda r: put_row(taps, r + 1, masked(low[row_at(r), :], q[row_at(r), :]), mk))
    put_halo(
        taps, masked(low[rows * COLS : (rows + 1) * COLS, :], recv[0:COLS, :]), mk, info, rows
    )
    conv_finish(rows, info, w, y, pay, None, taps, acc)


def turn_kernel(
    rows, info, cnt, y, stats, gain, bias, cot, pool, g, pay, acc, co, buf
):
    acc[...] = jnp.zeros_like(acc)
    norm_coefs(co, 0, stats, gain, bias, cnt, info)
    half = COLS // 2

    def pair(i):
        part = pl.ds(pl.multiple_of(i * half, half), half)
        ct = spread(buf, cot[part, :])
        total = None
        for k in range(2):
            here = row_at(2 * i + k)
            row = y[here, :]
            v = affine(row, co, 0, 1)
            s = sigmoid(v)
            f = v * s
            total = f if total is None else total + f
            gr = ct * (s * (1.0 + v * (1.0 - s)))
            g[here, :] = gr
            add_sums(acc, 0, gr)
            add_sums(acc, 1, gr * affine(row, co, 2, 3))
        pool[part, :] = pooled(buf, total).astype(BF)

    loop(rows // 2, pair)
    put_edge(pay, g, info, rows)
    put_sums(acc, info, pay, COLS)


def branch_back_kernel(
    rows, info, cnt, g, y, recv_g, recv_y, stats, sums, gain, bias, w, low, q, qstats, qgain, qbias,
    e, gq, gs, pay, taps, mk, acc, co,
):
    make_masks(mk, info)
    acc[...] = jnp.zeros_like(acc)
    norm_coefs(co, 0, stats, gain, bias, cnt, info)
    grad_coefs(co, 4, 0, sums, cnt, info)
    norm_coefs(co, 6, qstats, qgain, qbias, cnt, info)

    def each(r):
        row = grad_row(g[row_at(r), :], y[row_at(r), :], co, 0, 4)
        e[row_at(r), :] = row.astype(BF)
        put_row(taps, r + 1, row, mk)

    loop(rows, each)
    put_halo(taps, grad_row(recv_g[0:COLS, :], recv_y[0:COLS, :], co, 0, 4), mk, info, rows)

    def tile(m):
        gq[tile_at(m, TILE_ROWS), :] = conv_tile(taps, w, m * TILE_ROWS, TILE_ROWS, True)

    loop(rows // TILE_ROWS, tile)

    def post(r):
        here = row_at(r)
        grad = gq[here, :]
        row = q[here, :]
        gate = sigmoid(affine(row, co, 6, 7))
        gs[here, :] = grad * gate
        out = grad * low[here, :].astype(F32) * gate * (1.0 - gate)
        gq[here, :] = out
        add_sums(acc, 0, out)
        add_sums(acc, 1, out * affine(row, co, 8, 9))

    loop(rows, post)
    put_sums(acc, info, pay, 0)


def mask_back_kernel(
    rows, info, cnt, g, q, stats, sums, gain, bias, w, u, ustats, ugain, ubias, e, gu, pay, acc, co
):
    acc[...] = jnp.zeros_like(acc)
    norm_coefs(co, 0, stats, gain, bias, cnt, info)
    grad_coefs(co, 4, 0, sums, cnt, info)
    norm_coefs(co, 6, ustats, ugain, ubias, cnt, info)

    def each(r):
        e[row_at(r), :] = grad_row(g[row_at(r), :], q[row_at(r), :], co, 0, 4).astype(BF)

    loop(rows, each)

    def tile(m):
        here = tile_at(m, TILE_ROWS)
        gu[here, :] = jnp.dot(e[here, :], w[...], preferred_element_type=F32)

    loop(rows // TILE_ROWS, tile)

    def post(r):
        here = row_at(r)
        row = u[here, :]
        out = gu[here, :] * silu_slope(affine(row, co, 6, 7))
        gu[here, :] = out
        add_sums(acc, 0, out)
        add_sums(acc, 1, out * affine(row, co, 8, 9))

    loop(rows, post)
    put_sums(acc, info, pay, 0)


def leave_kernel(
    rows, info, cnt, g, u, stats, sums, gain, bias, w, gs, z, zstats, zgain, zbias, cot,
    e, out, pay, acc, co, buf, wide,
):
    acc[...] = jnp.zeros_like(acc)
    norm_coefs(co, 0, stats, gain, bias, cnt, info)
    grad_coefs(co, 4, 0, sums, cnt, info)
    norm_coefs(co, 6, zstats, zgain, zbias, cnt, info)

    def each(r):
        e[row_at(r), :] = grad_row(g[row_at(r), :], u[row_at(r), :], co, 0, 4).astype(BF)

    loop(rows, each)

    def tile(m):
        here = tile_at(m, TILE_ROWS)
        wide[here, :] = gs[here, :] + jnp.dot(e[here, :], w[...], preferred_element_type=F32)

    loop(rows // TILE_ROWS, tile)
    half = COLS // 2
    active = info[8] == 1

    def post(i):
        ct = spread(buf, cot[pl.ds(pl.multiple_of(i * half, half), half), :])
        for k in range(2):
            here = row_at(2 * i + k)
            grad = jnp.where(active, wide[here, :], ct)
            out[here, :] = grad.astype(BF)
            row = z[here, :]
            grad = grad * silu_slope(affine(row, co, 6, 7))
            add_sums(acc, 0, grad)
            add_sums(acc, 1, grad * affine(row, co, 8, 9))

    loop(rows // 2, post)
    put_sums(acc, info, pay, 0)


def trunk_back_kernel(
    rows, top, last, info, cnt, g, z, recv_g, recv_z, stats, sums, gain, bias, w, *rest
):
    if last:
        e, out, taps, mk, co = rest
    else:
        x, xstats, xgain, xbias, e, out, pay, taps, mk, co, acc = rest
        acc[...] = jnp.zeros_like(acc)
        norm_coefs(co, 6, xstats, xgain, xbias, cnt, info)
    make_masks(mk, info)
    norm_coefs(co, 0, stats, gain, bias, cnt, info)
    grad_coefs(co, 4, 0, sums, cnt, info)

    def grad(g_row, z_row):
        if top:
            g_row = g_row.astype(F32) * silu_slope(affine(z_row, co, 0, 1))
        return grad_row(g_row, z_row, co, 0, 4)

    def each(r):
        row = grad(g[row_at(r), :], z[row_at(r), :])
        e[row_at(r), :] = row.astype(BF)
        put_row(taps, r + 1, row, mk)

    loop(rows, each)
    put_halo(taps, grad(recv_g[0:COLS, :], recv_z[0:COLS, :]), mk, info, rows)

    def tile(m):
        out[tile_at(m, TILE_ROWS), :] = conv_tile(taps, w, m * TILE_ROWS, TILE_ROWS, True)

    loop(rows // TILE_ROWS, tile)
    if last:
        return

    def post(r):
        here = row_at(r)
        row = x[here, :]
        value = out[here, :] * silu_slope(affine(row, co, 6, 7))
        out[here, :] = value
        add_sums(acc, 0, value)
        add_sums(acc, 1, value * affine(row, co, 8, 9))

    loop(rows, post)
    put_edge(pay, out, info, rows)
    put_sums(acc, info, pay, COLS)


def trunk_wgrad_kernel(rows, quarter, e, out):
    width = rows * COLS
    wide = jnp.concatenate(
        [quarter[t % 3, (t // 3) * COLS : (t // 3) * COLS + width, :] for t in range(TAPS)], axis=1
    )
    out[...] = lax.dot_general(e[...], wide, TN, preferred_element_type=F32).astype(BF)


def branch_wgrad_kernel(rows, taps, ey, p, eq, low, eu, out):
    width = rows * COLS
    channels = ey.shape[1]
    for t in range(TAPS):
        di, dj = divmod(t, 3)
        a = taps[dj, di * COLS : di * COLS + width, :]
        out[:, t * channels : (t + 1) * channels] = lax.dot_general(
            ey[...], a, TN, preferred_element_type=F32
        ).astype(BF)
    out[:, 9 * channels : 10 * channels] = lax.dot_general(
        eu[...], low[0:width, :], TN, preferred_element_type=F32
    ).astype(BF)
    out[:, 10 * channels : 11 * channels] = lax.dot_general(
        eq[...], p[...], TN, preferred_element_type=F32
    ).astype(BF)


def run(kernel, ins, outs, scratch, limit, flops=0):
    specs = [SMEM if a.ndim == 1 else VMEM for a in ins]
    size = sum(a.size * a.dtype.itemsize for a in ins) + sum(
        o.size * o.dtype.itemsize for o in outs
    )
    return pl.pallas_call(
        kernel,
        out_shape=outs,
        in_specs=specs,
        out_specs=[VMEM] * len(outs),
        scratch_shapes=scratch,
        compiler_params=pltpu.CompilerParams(vmem_limit_bytes=limit * MIB),
        cost_estimate=pl.CostEstimate(flops=flops, bytes_accessed=size, transcendentals=0),
    )(*ins)


def swap(value, axis, mask):
    pairs = [(i, i ^ mask) for i in range(lax.axis_size(axis))]
    return lax.ppermute(value, axis, pairs)


def sum_over(value, axis, start=1):
    mask = start
    while mask < lax.axis_size(axis):
        value = value + swap(value, axis, mask)
        mask *= 2
    return value


def exchange(pay):
    recv = swap(pay, "dp", 1)
    return recv, sum_over(pay[COLS:] + recv[COLS:], "dp", 2)


def domain_counts(size_class, domain_tags):
    big_area = HEIGHT * WIDTH
    small_area = BAND * HALF_WIDTH
    ones_count = jnp.sum(
        jnp.where(
            size_class == 0, big_area * domain_tags[:, 0], small_area * jnp.sum(domain_tags, axis=1)
        )
    )
    all_count = size_class.shape[0] * big_area
    return jnp.maximum(jnp.stack([all_count - ones_count, ones_count]).astype(F32), 1.0)


def on_device(
    images,
    conv_first,
    conv_second,
    conv_third,
    trunk_gains,
    trunk_biases,
    attend_in,
    attend_mask,
    attend_out,
    branch_gains,
    branch_biases,
    size_class,
    domain_tags,
    trunk_cotangent,
    task_cotangent,
):
    rows, cols, ch = images.shape
    pixels = rows * cols
    position = lax.axis_index("dp")
    task_index = lax.axis_index("task")
    task_count = lax.axis_size("task")
    quarter = ch // task_count
    pair_index = position // 2
    bottom = position % 2
    local_class = lax.dynamic_slice_in_dim(size_class, pair_index * CANVAS, CANVAS, 0)
    local_tags = lax.dynamic_slice_in_dim(domain_tags, pair_index * CANVAS, CANVAS, 0)
    side = jnp.arange(GROUPS) % 2
    slot_class = jnp.repeat(local_class, 2)
    slot_tags = jnp.repeat(local_tags, 2, axis=0)
    which = jnp.where(slot_class == 1, bottom * 2 + side, 0)
    groups = jnp.sum(slot_tags * (jnp.arange(4)[None, :] == which[:, None]), axis=1)
    active = (task_index < TASKS).astype(jnp.int32)
    info = jnp.concatenate(
        [groups, local_class, jnp.stack([bottom, task_index, active])]
    ).astype(jnp.int32)
    cnt = domain_counts(size_class, domain_tags)

    def own(kernel):
        return jnp.transpose(kernel.reshape(-1, kernel.shape[-1])).astype(BF)

    branch = jnp.minimum(task_index, TASKS - 1)

    def pick(values):
        return lax.dynamic_index_in_dim(values, branch, 0, keepdims=False)

    gather = functools.partial(lax.all_gather, axis_name="dp", axis=0, tiled=True)
    weights = [gather(own(k)) for k in (conv_first, conv_second, conv_third)]
    w_in = gather(own(pick(attend_in)))
    w_mask = gather(own(pick(attend_mask)))
    w_out = gather(own(pick(attend_out)))
    gains = [trunk_gains[i : i + 1] for i in range(3)]
    biases = [trunk_biases[i : i + 1] for i in range(3)]
    own_gains = pick(branch_gains)
    own_biases = pick(branch_biases)
    b_gains = [own_gains[i : i + 1] for i in range(3)]
    b_biases = [own_biases[i : i + 1] for i in range(3)]

    def shape(dims, dtype=F32):
        return jax.ShapeDtypeStruct(dims, dtype)

    wide = shape((pixels, ch))
    low_wide = shape((pixels, ch), BF)
    pay_shape = shape((COLS + 8, ch))
    sums_shape = shape((8, ch))
    taps_dims = (3, pixels + 2 * COLS, ch)
    taps = pltpu.VMEM(taps_dims, BF)
    masks = pltpu.VMEM((2, COLS, 128), F32)
    acc = pltpu.VMEM((2, GROUPS, 8, ch), F32)
    buf = pltpu.VMEM((ch // 128, COLS, 128), F32)

    def coefs(blocks):
        return pltpu.VMEM((4 * blocks, ch), F32)

    conv_flops = 2 * TAPS * pixels * ch * ch
    dot_flops = 2 * pixels * ch * ch

    flat = images.reshape(pixels, ch)
    edge = jnp.where(bottom == 1, flat[:COLS], flat[pixels - COLS :])
    halo = swap(edge, "dp", 1)
    quarter_shape = shape((3, pixels + 2 * COLS, quarter), BF)
    z, recv, stats, quarters = [], [], [], []
    for layer in range(3):
        outs = [wide, pay_shape, quarter_shape]
        if layer == 0:
            values, pay, part = run(
                functools.partial(first_conv_kernel, rows),
                [info, flat, halo, weights[0]],
                outs, [taps, masks, acc], 30, conv_flops,
            )
        else:
            values, pay, part = run(
                functools.partial(conv_kernel, rows),
                [info, cnt, z[-1], recv[-1], stats[-1], gains[layer - 1], biases[layer - 1], weights[layer]],
                outs, [taps, masks, acc, coefs(4)], 30, conv_flops,
            )
        got, total = exchange(pay)
        z.append(values)
        recv.append(got)
        stats.append(total)
        quarters.append(part)

    low, trunk_pool, u, pay = run(
        functools.partial(enter_kernel, rows),
        [info, cnt, z[2], recv[2], stats[2], gains[2], biases[2], w_in],
        [shape((pixels + COLS, ch), BF), shape((pixels // 4, ch), BF), wide, sums_shape],
        [acc, coefs(4), buf], 24, dot_flops,
    )
    u_stats = sum_over(pay, "dp")
    p, q, pay = run(
        functools.partial(mask_kernel, rows),
        [info, cnt, u, u_stats, b_gains[0], b_biases[0], w_mask],
        [low_wide, wide, pay_shape], [acc, coefs(4)], 24, dot_flops,
    )
    q_recv, q_stats = exchange(pay)
    y, pay, masked_taps = run(
        functools.partial(branch_conv_kernel, rows),
        [info, cnt, low, q, q_recv, q_stats, b_gains[1], b_biases[1], w_out],
        [wide, pay_shape, shape(taps_dims, BF)], [masks, acc, coefs(4)], 34, conv_flops,
    )
    y_recv, y_stats = exchange(pay)

    cot = pick(task_cotangent).reshape(pixels // 4, ch)
    branch_pool, g_y, pay = run(
        functools.partial(turn_kernel, rows),
        [info, cnt, y, y_stats, b_gains[2], b_biases[2], cot],
        [shape((pixels // 4, ch), BF), wide, pay_shape], [acc, coefs(4), buf], 24,
    )
    gy_recv, y_sums = exchange(pay)
    e_y, g_q, gs, pay = run(
        functools.partial(branch_back_kernel, rows),
        [info, cnt, g_y, y, gy_recv, y_recv, y_stats, y_sums, b_gains[2], b_biases[2], w_out, low, q, q_stats,
         b_gains[1], b_biases[1]],
        [low_wide, wide, wide, sums_shape], [taps, masks, acc, coefs(10)], 44, conv_flops,
    )
    q_sums = sum_over(pay, "dp")
    e_q, g_u, pay = run(
        functools.partial(mask_back_kernel, rows),
        [info, cnt, g_q, q, q_stats, q_sums, b_gains[1], b_biases[1], w_mask, u, u_stats, b_gains[0], b_biases[0]],
        [low_wide, wide, sums_shape], [acc, coefs(10)], 28, dot_flops,
    )
    u_sums = sum_over(pay, "dp")
    trunk_cot = trunk_cotangent.reshape(pixels // 4, ch)
    e_u, grad_shared, pay = run(
        functools.partial(leave_kernel, rows),
        [info, cnt, g_u, u, u_stats, u_sums, b_gains[0], b_biases[0], w_in, gs, z[2], stats[2], gains[2],
         biases[2], trunk_cot],
        [low_wide, low_wide, sums_shape], [acc, coefs(10), buf, pltpu.VMEM((pixels, ch), F32)], 34, dot_flops,
    )
    sums = sum_over(sum_over(pay, "dp"), "task")
    grad_shared = lax.psum(grad_shared, "task")
    (branch_kernel_grad,) = run(
        functools.partial(branch_wgrad_kernel, rows),
        [masked_taps, e_y, p, e_q, low, e_u],
        [shape((ch, 11 * ch), BF)], [], 40, conv_flops,
    )

    edge = jnp.where(bottom == 1, grad_shared[:COLS], grad_shared[pixels - COLS :])
    g, g_recv = grad_shared, swap(edge, "dp", 1)
    kernel_parts = [None, None, None]
    trunk_sums = [None, None, None]
    for layer in (2, 1, 0):
        trunk_sums[layer] = sums
        last = layer == 0
        ins = [info, cnt, g, z[layer], g_recv, recv[layer], stats[layer], sums, gains[layer], biases[layer],
               weights[layer]]
        outs = [low_wide, wide]
        scratch = [taps, masks, coefs(10)]
        if not last:
            ins += [z[layer - 1], stats[layer - 1], gains[layer - 1], biases[layer - 1]]
            outs += [pay_shape]
            scratch += [acc]
        got = run(
            functools.partial(trunk_back_kernel, rows, layer == 2, last),
            ins, outs, scratch, 38, conv_flops,
        )
        e, g = got[0], got[1]
        (kernel_parts[layer],) = run(
            functools.partial(trunk_wgrad_kernel, rows),
            [quarters[layer], e], [shape((ch, TAPS * quarter), BF)], [], 24, conv_flops // 4,
        )
        if not last:
            g_recv, sums = exchange(got[2])

    def scatter(values):
        return lax.psum_scatter(values, "dp", scatter_dimension=0, tiled=True)

    def collect(values):
        return lax.all_gather(values, "task", axis=0, tiled=False)

    task_features = collect(branch_pool)[:TASKS].reshape(TASKS, rows // 2, cols // 2, ch)
    trunk_kernel_grads = []
    for part in kernel_parts:
        whole = collect(scatter(part))
        outc = whole.shape[1]
        whole = whole.reshape(task_count, outc, TAPS, quarter).transpose(2, 0, 3, 1)
        trunk_kernel_grads.append(whole.astype(F32).reshape(3, 3, ch, outc))
    whole = collect(scatter(branch_kernel_grad))[:TASKS]
    outc = whole.shape[1]
    whole = whole.reshape(TASKS, outc, 11, ch).transpose(0, 2, 3, 1).astype(F32)
    out_grad = whole[:, :TAPS].reshape(TASKS, 3, 3, ch, outc)
    in_grad = whole[:, TAPS]
    mask_grad = whole[:, TAPS + 1]
    branch_sums = collect(jnp.stack([u_sums[:4], q_sums[:4], y_sums[:4]]))[:TASKS]
    trunk_sums = jnp.stack([s[:4] for s in trunk_sums])
    return (
        trunk_pool.reshape(rows // 2, cols // 2, ch),
        task_features,
        g.reshape(rows, cols, ch),
        trunk_kernel_grads[0],
        trunk_kernel_grads[1],
        trunk_kernel_grads[2],
        trunk_sums[:, 2] + trunk_sums[:, 3],
        trunk_sums[:, 0] + trunk_sums[:, 1],
        in_grad,
        mask_grad,
        out_grad,
        branch_sums[:, :, 2] + branch_sums[:, :, 3],
        branch_sums[:, :, 0] + branch_sums[:, :, 1],
    )


def solution(mesh):
    in_specs = (
        P("dp", None, None),
        P(None, None, None, "dp"),
        P(None, None, None, "dp"),
        P(None, None, None, "dp"),
        P(),
        P(),
        P(None, None, "dp"),
        P(None, None, "dp"),
        P(None, None, None, None, "dp"),
        P(),
        P(),
        P(),
        P(),
        P("dp", None, None),
        P(None, "dp", None, None),
    )
    out_specs = (
        P("dp", None, None),
        P(None, "dp", None, None),
        P("dp", None, None),
        P(None, None, None, "dp"),
        P(None, None, None, "dp"),
        P(None, None, None, "dp"),
        P(),
        P(),
        P(None, None, "dp"),
        P(None, None, "dp"),
        P(None, None, None, None, "dp"),
        P(),
        P(),
    )
    return jax.shard_map(
        on_device, mesh=mesh, in_specs=in_specs, out_specs=out_specs, check_vma=False
    )
```

```python
import functools
import math

import jax
import jax.numpy as jnp
from jax import lax
from jax.experimental import pallas as pl
from jax.experimental.pallas import tpu as pltpu
from jax.sharding import PartitionSpec as P

HEIGHT = 36
WIDTH = 48
BAND = 18
HALF_WIDTH = 24
CANVAS = 2
TASKS = 3
COLS = CANVAS * WIDTH
GROUPS = COLS // HALF_WIDTH
EPSILON = 1e-05
TAPS = 9
TILE_ROWS = 6
PIECE = 16
MIB = 2**20
BF = jnp.bfloat16
F32 = jnp.float32
NT = (((1,), (1,)), ((), ()))
TN = (((0,), (0,)), ((), ()))

ANY = pl.BlockSpec(memory_space=pl.ANY)
HBM = pl.BlockSpec(memory_space=pltpu.HBM)
SMEM = pl.BlockSpec(memory_space=pltpu.SMEM)


def affine(row, co, scale, shift):
    step = row.shape[0] // GROUPS
    return jnp.concatenate(
        [
            row[step * j : step * (j + 1)] * co[4 * scale + j : 4 * scale + j + 1, :]
            + co[4 * shift + j : 4 * shift + j + 1, :]
            for j in range(GROUPS)
        ],
        axis=0,
    )


def scaled(row, co, scale):
    step = row.shape[0] // GROUPS
    return jnp.concatenate(
        [
            row[step * j : step * (j + 1)] * co[4 * scale + j : 4 * scale + j + 1, :]
            for j in range(GROUPS)
        ],
        axis=0,
    )


def sigmoid(v):
    return 0.5 * jnp.tanh(0.5 * v) + 0.5


def silu(v):
    return v * sigmoid(v)


def silu_slope(v):
    s = sigmoid(v)
    return s * (1.0 + v * (1.0 - s))


def norm_coefs(co, base, stats, params, which, cnt, info):
    gain = params[which : which + 1, :]
    bias = params[which + 6 : which + 7, :]
    means, scales = [], []
    for d in range(2):
        mean = stats[d : d + 1, :] / cnt[d]
        var = stats[2 + d : 3 + d, :] / cnt[d] - mean * mean
        means.append(mean)
        scales.append(lax.rsqrt(var + EPSILON))
    for j in range(GROUPS):
        one = info[j] == 1
        mean = jnp.where(one, means[1], means[0])
        scale = jnp.where(one, scales[1], scales[0])
        full = scale * gain
        co[4 * base + j : 4 * base + j + 1, :] = full
        co[4 * base + 4 + j : 4 * base + 5 + j, :] = bias - mean * full
        co[4 * base + 8 + j : 4 * base + 9 + j, :] = scale
        co[4 * base + 12 + j : 4 * base + 13 + j, :] = -mean * scale


def grad_coefs(co, base, norm, sums, cnt, info):
    for j in range(GROUPS):
        one = info[j] == 1
        count = jnp.where(one, cnt[1], cnt[0])
        plain = jnp.where(one, sums[1:2, :], sums[0:1, :]) / count
        cross = jnp.where(one, sums[3:4, :], sums[2:3, :]) / count
        full = co[4 * norm + j : 4 * norm + j + 1, :]
        scale = co[4 * norm + 8 + j : 4 * norm + 9 + j, :]
        shift = co[4 * norm + 12 + j : 4 * norm + 13 + j, :]
        co[4 * base + j : 4 * base + j + 1, :] = -full * cross * scale
        co[4 * base + 4 + j : 4 * base + 5 + j, :] = -full * (plain + cross * shift)


def grad_row(g, z, co, norm, base):
    return scaled(g, co, norm) + affine(z, co, base, base + 1)


def add_sums(acc, slot, values):
    step = HALF_WIDTH // 8
    count = values.shape[0] // COLS
    channels = values.shape[1]
    acc[slot] += jnp.sum(
        values.reshape(count, GROUPS, step, 8, channels), axis=(0, 2)
    )


def put_sums(acc, info, out, start):
    for slot in range(2):
        groups = [jnp.sum(acc[slot, j], axis=0, keepdims=True) for j in range(GROUPS)]
        for d in range(2):
            total = jnp.zeros_like(groups[0])
            for j in range(GROUPS):
                total = total + jnp.where(info[j] == d, groups[j], 0.0)
            row = start + 2 * slot + d
            out[row : row + 1, :] = total
    out[start + 4 : start + 8, :] = jnp.zeros((4, out.shape[1]), F32)


def put_edge(out, ref, info, rows):
    start = jnp.where(info[6] == 1, 0, (rows - 1) * COLS)
    out[0:COLS, :] = ref[pl.ds(pl.multiple_of(start, COLS), COLS), :].astype(out.dtype)


def make_masks(mk, info):
    col = lax.broadcasted_iota(jnp.int32, mk.shape[1:], 0)
    small = (info[4] == 1, info[5] == 1)
    left = (col == 0) | (col == WIDTH)
    right = (col == WIDTH - 1) | (col == COLS - 1)
    for s in range(2):
        left = left | ((col == s * WIDTH + HALF_WIDTH) & small[s])
        right = right | ((col == s * WIDTH + HALF_WIDTH - 1) & small[s])
    mk[0] = jnp.where(left, 0.0, 1.0)
    mk[1] = jnp.where(right, 0.0, 1.0)


def put_row(taps, at, row, mk):
    parts = row.shape[1] // mk.shape[2]
    left = jnp.concatenate([mk[0]] * parts, axis=1)
    right = jnp.concatenate([mk[1]] * parts, axis=1)
    here = pl.ds(pl.multiple_of(at * COLS, COLS), COLS)
    taps[0, here, :] = (pltpu.roll(row, 1, 0) * left).astype(BF)
    taps[1, here, :] = row.astype(BF)
    taps[2, here, :] = (pltpu.roll(row, COLS - 1, 0) * right).astype(BF)


def put_halo(taps, row, mk, info, rows):
    step = COLS // GROUPS
    keep = [jnp.where(info[4 + j // 2] == 1, 0.0, 1.0) for j in range(GROUPS)]
    row = jnp.concatenate(
        [row[step * j : step * (j + 1)] * keep[j] for j in range(GROUPS)], axis=0
    )
    put_row(taps, jnp.where(info[6] == 1, 0, rows + 1), row, mk)
    put_row(taps, jnp.where(info[6] == 1, rows + 1, 0), jnp.zeros_like(row), mk)


def conv_tile(taps, w, at, rows, transpose):
    acc = None
    channels = taps.shape[2]
    for t in range(TAPS):
        di, dj = divmod(t, 3)
        a = taps[dj, (at + di) * COLS : (at + di + rows) * COLS, :]
        if transpose:
            k = w[:, (8 - t) * channels : (9 - t) * channels]
            r = jnp.dot(a, k, preferred_element_type=F32)
        else:
            k = w[:, t * channels : (t + 1) * channels]
            r = lax.dot_general(a, k, NT, preferred_element_type=F32)
        acc = r if acc is None else acc + r
    return acc


def row_at(r):
    return pl.ds(pl.multiple_of(r * COLS, COLS), COLS)


def tile_at(m):
    return slice(m * TILE_ROWS * COLS, (m + 1) * TILE_ROWS * COLS)


def loop(count, body):
    def step(i, carry):
        body(i)
        return carry

    lax.fori_loop(0, count, step, 0)


def pooled(buf, values):
    half = COLS // 2
    parts, _, lanes = buf.shape
    out = []
    for c in range(parts):
        buf[c] = values[:, c * lanes : (c + 1) * lanes]
        out.append(buf[c, pl.ds(0, half, stride=2), :] + buf[c, pl.ds(1, half, stride=2), :])
    return jnp.concatenate(out, axis=1) * 0.25


def spread(buf, values):
    half = COLS // 2
    parts, _, lanes = buf.shape
    quarter = values.astype(F32) * 0.25
    out = []
    for c in range(parts):
        part = quarter[:, c * lanes : (c + 1) * lanes]
        buf[c, pl.ds(0, half, stride=2), :] = part
        buf[c, pl.ds(1, half, stride=2), :] = part
        out.append(buf[c])
    return jnp.concatenate(out, axis=1)


class Copies:
    def __init__(self, sems):
        self.sems = sems
        self.used = 0
        self.open = []

    def start(self, src, dst):
        copy = pltpu.make_async_copy(src, dst, self.sems.at[self.used])
        self.used += 1
        copy.start()
        return copy

    def put(self, src, dst):
        self.open.append(self.start(src, dst))

    def tiles(self, src, dst, rows):
        return [
            self.start(src.at[pl.ds(m * TILE_ROWS * COLS, TILE_ROWS * COLS)],
                       dst.at[pl.ds(m * TILE_ROWS * COLS, TILE_ROWS * COLS)])
            for m in range(rows // TILE_ROWS)
        ]

    def put_tile(self, src, dst, m):
        here = pl.ds(m * TILE_ROWS * COLS, TILE_ROWS * COLS)
        self.put(src.at[here], dst.at[here])

    def weights(self, pieces, place, dst):
        if len(pieces) == 1:
            return [self.start(pieces[0], dst)]
        copies = []
        count = pieces[0].shape[0] // PIECE
        for i, piece in enumerate(pieces):
            for k in range(count):
                row = pl.multiple_of(place[i * count + k], PIECE)
                copies.append(
                    self.start(piece.at[pl.ds(k * PIECE, PIECE)], dst.at[pl.ds(row, PIECE)])
                )
        return copies

    def finish(self):
        for copy in self.open:
            copy.wait()


def fetch_sums(io, sums, dst):
    return [io.start(part, dst.at[k]) for k, part in enumerate(sums)]


def settle(dst, count):
    if count == 4:
        dst[0] = (dst[0] + dst[1]) + (dst[2] + dst[3])
    return dst.at[0]


def wait(*copies):
    for copy in copies:
        copy.wait()


def tile_rows(m):
    return range(m * TILE_ROWS, (m + 1) * TILE_ROWS)


def each_row(m, body):
    loop(TILE_ROWS, lambda r: body(m * TILE_ROWS + r))


def cast_kernel(pick, count, spot, *refs):
    sources, out, wide, sems = refs[:count], refs[-count - 2], refs[-count - 1 : -1], refs[-1]
    io = Copies(sems)
    rows, channels = out.shape[0], wide[0].shape[2]
    first = pl.multiple_of(spot[0] * rows, rows) if pick else 0
    reads = []
    for src, dst in zip(sources, wide):
        if len(src.shape) == 4:
            src = src.at[spot[1]]
        reads.append(io.start(src.at[:, pl.ds(first, rows), :], dst))
    start = 0
    for src, read in zip(wide, reads):
        read.wait()
        for t in range(src.shape[0]):
            out[:, start : start + channels] = src[t].astype(BF)
            start += channels


def conv_outputs(rows, info, w, z, zv, pay, payv, quarter, taps, acc, io, w_reads):
    if quarter is not None:
        width = quarter.shape[2]
        io.put(taps.at[:, :, pl.ds(pl.multiple_of(info[7] * width, 128), width)], quarter)
    wait(*w_reads)
    for m in range(rows // TILE_ROWS):
        out = conv_tile(taps, w, m * TILE_ROWS, TILE_ROWS, False)
        zv[tile_at(m), :] = out
        io.put_tile(zv, z, m)
        add_sums(acc, 0, out)
        add_sums(acc, 1, out * out)
    put_edge(payv, zv, info, rows)
    put_sums(acc, info, payv, COLS)
    io.put(payv, pay)


def first_conv_kernel(rows, info, place, x, halo, pieces, z, zv, pay, quarter, xv, hv, payv, wv, taps, mk, acc, sems):
    io = Copies(sems)
    reads = io.tiles(x, xv, rows)
    halo_read = io.start(halo, hv)
    w_reads = io.weights(pieces, place, wv)
    make_masks(mk, info)
    acc[...] = jnp.zeros_like(acc)
    for m, read in enumerate(reads):
        read.wait()
        each_row(m, lambda r: put_row(taps, r + 1, xv[row_at(r), :].astype(F32), mk))
    halo_read.wait()
    put_halo(taps, hv[...].astype(F32), mk, info, rows)
    conv_outputs(rows, info, wv, z, zv, pay, payv, quarter, taps, acc, io, w_reads)
    io.finish()


def conv_kernel(
    rows, which, info, cnt, place, params, x, recv, stats, pieces, z, zv, pay, quarter,
    pv, hv, sv, payv, wv, taps, mk, acc, co, sems,
):
    io = Copies(sems)
    small = [*fetch_sums(io, stats, sv), io.start(params, pv)]
    halo_read = io.start(recv, hv)
    w_reads = io.weights(pieces, place, wv)
    make_masks(mk, info)
    acc[...] = jnp.zeros_like(acc)
    wait(*small)
    norm_coefs(co, 0, settle(sv, len(stats)), pv, which, cnt, info)
    loop(rows, lambda r: put_row(taps, r + 1, silu(affine(x[row_at(r), :], co, 0, 1)), mk))
    halo_read.wait()
    put_halo(taps, silu(affine(hv[0:COLS, :], co, 0, 1)), mk, info, rows)
    conv_outputs(rows, info, wv, z, zv, pay, payv, quarter, taps, acc, io, w_reads)
    io.finish()


def enter_kernel(
    rows, which, info, cnt, params, x, recv, stats, w, low, pool, u, uv, pay,
    pv, hv, sv, wv, lowv, poolv, payv, acc, co, buf, sems,
):
    io = Copies(sems)
    small = [*fetch_sums(io, stats, sv), io.start(params, pv)]
    halo_read = io.start(recv, hv)
    w_read = io.start(w.at[:, pl.ds(0, wv.shape[1])], wv)
    acc[...] = jnp.zeros_like(acc)
    wait(*small)
    norm_coefs(co, 0, settle(sv, len(stats)), pv, which, cnt, info)
    half = COLS // 2

    def pair(i):
        first = silu(affine(x[row_at(2 * i), :], co, 0, 1))
        second = silu(affine(x[row_at(2 * i + 1), :], co, 0, 1))
        lowv[row_at(2 * i), :] = first.astype(BF)
        lowv[row_at(2 * i + 1), :] = second.astype(BF)
        poolv[pl.ds(pl.multiple_of(i * half, half), half), :] = pooled(
            buf, first + second
        ).astype(BF)

    halo_read.wait()
    lowv[rows * COLS : (rows + 1) * COLS, :] = silu(affine(hv[0:COLS, :], co, 0, 1)).astype(BF)
    for m in range(rows // TILE_ROWS):
        loop(TILE_ROWS // 2, lambda i: pair(m * (TILE_ROWS // 2) + i))
        if m == 0:
            w_read.wait()
        out = lax.dot_general(lowv[tile_at(m), :], wv[...], NT, preferred_element_type=F32)
        uv[tile_at(m), :] = out
        io.put_tile(uv, u, m)
        add_sums(acc, 0, out)
        add_sums(acc, 1, out * out)
    io.put(lowv, low)
    io.put(poolv, pool)
    put_sums(acc, info, payv, 0)
    io.put(payv, pay)
    io.finish()


def mask_kernel(
    rows, which, info, cnt, params, u, stats, w, p, q, qv, pay, pv, sv, wv, ev, payv, acc, co, sems
):
    io = Copies(sems)
    small = [*fetch_sums(io, stats, sv), io.start(params, pv)]
    w_read = io.start(w.at[:, pl.ds(wv.shape[1], wv.shape[1])], wv)
    acc[...] = jnp.zeros_like(acc)
    wait(*small)
    norm_coefs(co, 0, settle(sv, len(stats)), pv, which, cnt, info)

    def each(r):
        ev[row_at(r), :] = silu(affine(u[row_at(r), :], co, 0, 1)).astype(BF)

    for m in range(rows // TILE_ROWS):
        each_row(m, each)
        io.put_tile(ev, p, m)
        if m == 0:
            w_read.wait()
        out = lax.dot_general(ev[tile_at(m), :], wv[...], NT, preferred_element_type=F32)
        qv[tile_at(m), :] = out
        io.put_tile(qv, q, m)
        add_sums(acc, 0, out)
        add_sums(acc, 1, out * out)
    put_edge(payv, qv, info, rows)
    put_sums(acc, info, payv, COLS)
    io.put(payv, pay)
    io.finish()


def branch_conv_kernel(
    rows, which, info, cnt, params, low, q, recv, stats, w, y, yv, pay, wide_taps,
    pv, lv, hv, sv, payv, wv, taps, mk, acc, co, sems,
):
    io = Copies(sems)
    small = [*fetch_sums(io, stats, sv), io.start(params, pv)]
    low_read = io.start(low, lv)
    halo_read = io.start(recv, hv)
    w_read = io.start(w, wv)
    make_masks(mk, info)
    acc[...] = jnp.zeros_like(acc)
    wait(*small)
    norm_coefs(co, 0, settle(sv, len(stats)), pv, which, cnt, info)

    def masked(source, gated):
        return source.astype(F32) * sigmoid(affine(gated, co, 0, 1))

    low_read.wait()
    loop(rows, lambda r: put_row(taps, r + 1, masked(lv[row_at(r), :], q[row_at(r), :]), mk))
    halo_read.wait()
    put_halo(taps, masked(lv[rows * COLS : (rows + 1) * COLS, :], hv[0:COLS, :]), mk, info, rows)
    io.put(taps, wide_taps)
    conv_outputs(rows, info, wv, y, yv, pay, payv, None, taps, acc, io, [w_read])
    io.finish()


def turn_kernel(
    rows, which, info, cnt, params, y, stats, cot, pool, gv, pay, pv, sv, cv, poolv, payv, acc, co, buf, sems
):
    io = Copies(sems)
    small = [*fetch_sums(io, stats, sv), io.start(params, pv)]
    cot_read = io.start(cot.at[info[9]], cv)
    acc[...] = jnp.zeros_like(acc)
    wait(*small)
    norm_coefs(co, 0, settle(sv, len(stats)), pv, which, cnt, info)
    half = COLS // 2

    def pair(i):
        part = pl.ds(pl.multiple_of(i * half, half), half)
        ct = spread(buf, cv[part, :])
        total = None
        for k in range(2):
            here = row_at(2 * i + k)
            row = y[here, :]
            v = affine(row, co, 0, 1)
            s = sigmoid(v)
            f = v * s
            total = f if total is None else total + f
            gr = ct * (s * (1.0 + v * (1.0 - s)))
            gv[here, :] = gr
            add_sums(acc, 0, gr)
            add_sums(acc, 1, gr * affine(row, co, 2, 3))
        poolv[part, :] = pooled(buf, total).astype(BF)

    cot_read.wait()
    loop(rows // 2, pair)
    io.put(poolv, pool)
    put_edge(payv, gv, info, rows)
    put_sums(acc, info, payv, COLS)
    io.put(payv, pay)
    io.finish()


def branch_back_kernel(
    rows, info, cnt, params, g, y, recv_g, recv_y, stats, sums, w, low, q, qstats,
    e, gv, gs, pay,
    pv, yv, hv, kv, sv, tv, qsv, lv, qv, ev, payv, wv, taps, mk, acc, co, sems,
):
    io = Copies(sems)
    small = [*fetch_sums(io, stats, sv), *fetch_sums(io, sums, tv), *fetch_sums(io, qstats, qsv),
             io.start(params, pv)]
    reads = io.tiles(y, yv, rows)
    halo_reads = [io.start(recv_g, hv), io.start(recv_y, kv)]
    w_read = io.start(w, wv)
    low_read = io.start(low.at[pl.ds(0, rows * COLS)], lv)
    q_read = io.start(q, qv)
    make_masks(mk, info)
    acc[...] = jnp.zeros_like(acc)
    wait(*small)
    norm_coefs(co, 0, settle(sv, len(stats)), pv, 5, cnt, info)
    grad_coefs(co, 4, 0, settle(tv, len(sums)), cnt, info)
    norm_coefs(co, 6, settle(qsv, len(qstats)), pv, 4, cnt, info)

    def each(r):
        row = grad_row(g[row_at(r), :], yv[row_at(r), :], co, 0, 4)
        ev[row_at(r), :] = row.astype(BF)
        put_row(taps, r + 1, row, mk)

    for m, read in enumerate(reads):
        read.wait()
        each_row(m, each)
        io.put_tile(ev, e, m)
    wait(*halo_reads)
    put_halo(taps, grad_row(hv[0:COLS, :], kv[0:COLS, :], co, 0, 4), mk, info, rows)
    wait(w_read, low_read, q_read)

    def post(r):
        here = row_at(r)
        grad = gv[here, :]
        row = qv[here, :]
        gate = sigmoid(affine(row, co, 6, 7))
        yv[here, :] = grad * gate
        out = grad * lv[here, :].astype(F32) * gate * (1.0 - gate)
        gv[here, :] = out
        add_sums(acc, 0, out)
        add_sums(acc, 1, out * affine(row, co, 8, 9))

    for m in range(rows // TILE_ROWS):
        gv[tile_at(m), :] = conv_tile(taps, wv, m * TILE_ROWS, TILE_ROWS, True)
        each_row(m, post)
        io.put_tile(yv, gs, m)
    put_sums(acc, info, payv, 0)
    io.put(payv, pay)
    io.finish()


def mask_back_kernel(
    rows, info, cnt, params, g, q, stats, sums, w, u, ustats, e, gv, pay,
    pv, qv, uv, sv, tv, usv, wv, ev, payv, acc, co, sems,
):
    io = Copies(sems)
    small = [*fetch_sums(io, stats, sv), *fetch_sums(io, sums, tv), *fetch_sums(io, ustats, usv),
             io.start(params, pv)]
    reads = io.tiles(q, qv, rows)
    w_read = io.start(w.at[:, pl.ds(wv.shape[1], wv.shape[1])], wv)
    u_reads = io.tiles(u, uv, rows)
    acc[...] = jnp.zeros_like(acc)
    wait(*small)
    norm_coefs(co, 0, settle(sv, len(stats)), pv, 4, cnt, info)
    grad_coefs(co, 4, 0, settle(tv, len(sums)), cnt, info)
    norm_coefs(co, 6, settle(usv, len(ustats)), pv, 3, cnt, info)

    def each(r):
        ev[row_at(r), :] = grad_row(g[row_at(r), :], qv[row_at(r), :], co, 0, 4).astype(BF)

    def post(r):
        here = row_at(r)
        row = uv[here, :]
        out = gv[here, :] * silu_slope(affine(row, co, 6, 7))
        gv[here, :] = out
        add_sums(acc, 0, out)
        add_sums(acc, 1, out * affine(row, co, 8, 9))

    for m, read in enumerate(reads):
        read.wait()
        each_row(m, each)
        io.put_tile(ev, e, m)
        if m == 0:
            w_read.wait()
        gv[tile_at(m), :] = jnp.dot(ev[tile_at(m), :], wv[...], preferred_element_type=F32)
        u_reads[m].wait()
        each_row(m, post)
    put_sums(acc, info, payv, 0)
    io.put(payv, pay)
    io.finish()


def leave_kernel(
    rows, info, cnt, params, g, u, stats, sums, w, gs, z, zstats, cot, e, out, pay,
    pv, gv, uv, sv, tv, zsv, wv, gsv, zv, cv, ev, ov, payv, acc, co, buf, sems,
):
    io = Copies(sems)
    small = [*fetch_sums(io, stats, sv), *fetch_sums(io, sums, tv), *fetch_sums(io, zstats, zsv),
             io.start(params, pv)]
    reads = io.tiles(u, uv, rows)
    w_read = io.start(w.at[:, pl.ds(0, wv.shape[1])], wv)
    later = list(zip(io.tiles(gs, gsv, rows), io.tiles(z, zv, rows)))
    cot_read = io.start(cot, cv)
    acc[...] = jnp.zeros_like(acc)
    wait(*small)
    norm_coefs(co, 0, settle(sv, len(stats)), pv, 3, cnt, info)
    grad_coefs(co, 4, 0, settle(tv, len(sums)), cnt, info)
    norm_coefs(co, 6, settle(zsv, len(zstats)), pv, 2, cnt, info)
    half = COLS // 2
    active = info[8] == 1

    def each(r):
        ev[row_at(r), :] = grad_row(g[row_at(r), :], uv[row_at(r), :], co, 0, 4).astype(BF)

    def post(i):
        ct = spread(buf, cv[pl.ds(pl.multiple_of(i * half, half), half), :])
        for k in range(2):
            here = row_at(2 * i + k)
            grad = jnp.where(active, gv[here, :] + gsv[here, :], ct)
            ov[here, :] = grad.astype(BF)
            row = zv[here, :]
            grad = grad * silu_slope(affine(row, co, 6, 7))
            add_sums(acc, 0, grad)
            add_sums(acc, 1, grad * affine(row, co, 8, 9))

    for m, read in enumerate(reads):
        read.wait()
        each_row(m, each)
        io.put_tile(ev, e, m)
        if m == 0:
            wait(w_read, cot_read)
        gv[tile_at(m), :] = jnp.dot(ev[tile_at(m), :], wv[...], preferred_element_type=F32)
        wait(*later[m])
        loop(TILE_ROWS // 2, lambda i: post(m * (TILE_ROWS // 2) + i))
        io.put_tile(ov, out, m)
    put_sums(acc, info, payv, 0)
    io.put(payv, pay)
    io.finish()


def trunk_back_kernel(
    rows, which, top, info, cnt, place, params, g, z, recv_g, recv_z, stats, sums, x, xstats, pieces,
    e, out, pay, pv, zv, hv, kv, sv, tv, xv, xsv, ev, payv, wv, taps, mk, co, acc, *rest
):
    io = Copies(rest[-1])
    small = [*fetch_sums(io, stats, sv), *fetch_sums(io, sums, tv), *fetch_sums(io, xstats, xsv),
             io.start(params, pv)]
    gv = rest[:-1] if top else (g,)
    reads = [io.tiles(z, zv, rows)]
    if top:
        reads += [io.tiles(a, b, rows) for a, b in zip(g, gv)]
    reads = list(zip(*reads))
    halo_reads = [io.start(recv_g, hv), io.start(recv_z, kv)]
    w_reads = io.weights(pieces, place, wv)
    x_reads = io.tiles(x, xv, rows)
    acc[...] = jnp.zeros_like(acc)
    make_masks(mk, info)
    wait(*small)
    norm_coefs(co, 0, settle(sv, len(stats)), pv, which, cnt, info)
    grad_coefs(co, 4, 0, settle(tv, len(sums)), cnt, info)
    norm_coefs(co, 6, settle(xsv, len(xstats)), pv, which - 1, cnt, info)

    def grad(g_row, z_row):
        if top:
            g_row = g_row * silu_slope(affine(z_row, co, 0, 1))
        return grad_row(g_row, z_row, co, 0, 4)

    def each(r):
        g_row = gv[0][row_at(r), :]
        if top:
            g_row = g_row.astype(F32) + gv[1][row_at(r), :].astype(F32)
        row = grad(g_row, zv[row_at(r), :])
        ev[row_at(r), :] = row.astype(BF)
        put_row(taps, r + 1, row, mk)

    for m, pair in enumerate(reads):
        wait(*pair)
        each_row(m, each)
        io.put_tile(ev, e, m)
    wait(*halo_reads)
    put_halo(taps, grad(hv[0:COLS, :].astype(F32), kv[0:COLS, :]), mk, info, rows)
    wait(*w_reads)

    def post(r):
        here = row_at(r)
        row = xv[here, :]
        value = out[here, :] * silu_slope(affine(row, co, 6, 7))
        out[here, :] = value
        add_sums(acc, 0, value)
        add_sums(acc, 1, value * affine(row, co, 8, 9))

    for m in range(rows // TILE_ROWS):
        out[tile_at(m), :] = conv_tile(taps, wv, m * TILE_ROWS, TILE_ROWS, True)
        x_reads[m].wait()
        each_row(m, post)
    put_edge(payv, out, info, rows)
    put_sums(acc, info, payv, COLS)
    io.put(payv, pay)
    io.finish()


def wide_quarter(rows, quarter):
    width = rows * COLS
    return jnp.concatenate(
        [quarter[t % 3, (t // 3) * COLS : (t // 3) * COLS + width, :] for t in range(TAPS)], axis=1
    )


def last_grad_kernel(
    rows, info, place, cnt, params, g, z, recv_g, recv_z, stats, sums, quarter,
    e, mine, other, pv, zv, hv, kv, sv, tv, av, ev, wv, co, sems,
):
    io = Copies(sems)
    small = [*fetch_sums(io, stats, sv), *fetch_sums(io, sums, tv), io.start(params, pv)]
    reads = io.tiles(z, zv, rows)
    halo_reads = [io.start(recv_g, hv), io.start(recv_z, kv)]
    a_read = io.start(quarter, av)
    wait(*small)
    norm_coefs(co, 0, settle(sv, len(stats)), pv, 0, cnt, info)
    grad_coefs(co, 4, 0, settle(tv, len(sums)), cnt, info)

    def each(r):
        ev[row_at(r + 1), :] = grad_row(g[row_at(r), :], zv[row_at(r), :], co, 0, 4).astype(BF)

    for m, read in enumerate(reads):
        read.wait()
        each_row(m, each)
    wait(*halo_reads)
    row = grad_row(hv[0:COLS, :], kv[0:COLS, :], co, 0, 4)
    step = COLS // GROUPS
    row = jnp.concatenate(
        [
            row[step * j : step * (j + 1)] * jnp.where(info[4 + j // 2] == 1, 0.0, 1.0)
            for j in range(GROUPS)
        ],
        axis=0,
    ).astype(BF)
    ev[row_at(jnp.where(info[6] == 1, 0, rows + 1)), :] = row
    ev[row_at(jnp.where(info[6] == 1, rows + 1, 0)), :] = jnp.zeros_like(row)
    io.put(ev, e)
    a_read.wait()
    wv[...] = lax.dot_general(
        ev[COLS : (rows + 1) * COLS, :], wide_quarter(rows, av), TN, preferred_element_type=F32
    ).astype(BF)
    if other is None:
        io.put(wv, mine)
    else:
        size = mine.shape[0] // 4
        for k, mask in enumerate((0, 2, 1, 3)):
            for side, dst in ((0, mine), (1, other)):
                block = info[10] ^ (2 * mask + side)
                src = wv.at[pl.ds(pl.multiple_of(block * size, size), size)]
                io.put(src, dst.at[pl.ds(k * size, size)])
    io.finish()


def whole_last_grad_kernel(rows, *refs):
    last_grad_kernel(rows, *refs[:13], None, *refs[13:])


def last_conv_kernel(m, info, place, e, pieces, *refs):
    out, ev, ov, wv, taps, mk, sems = refs[-7:]
    io = Copies(sems)
    high = TILE_ROWS + 2
    read = io.start(e.at[pl.ds(m * TILE_ROWS * COLS, high * COLS)], ev)
    w_reads = io.weights(pieces, place, wv)
    make_masks(mk, info)
    read.wait()
    loop(high, lambda r: put_row(taps, r, ev[row_at(r), :].astype(F32), mk))
    wait(*w_reads)
    ov[...] = conv_tile(taps, wv, 0, TILE_ROWS, True)
    io.put(ov, out.at[pl.ds(m * TILE_ROWS * COLS, TILE_ROWS * COLS)])
    io.finish()


def trunk_wgrad_kernel(rows, quarter, e, part, av, ev, ov, sems):
    io = Copies(sems)
    reads = [io.start(quarter, av), io.start(e, ev)]
    wait(*reads)
    ov[...] = lax.dot_general(ev[...], wide_quarter(rows, av), TN, preferred_element_type=F32).astype(BF)
    io.put(ov, part)
    io.finish()


def branch_wgrad_kernel(rows, taps, ey, p, eq, low, eu, out, tv, yv, pv, qv, lv, uv, ov, sems):
    width = rows * COLS
    channels = ey.shape[1]
    io = Copies(sems)
    y_read = io.start(ey, yv)
    t_reads = [io.start(taps.at[k], tv.at[k]) for k in range(3)]
    reads = [io.start(p, pv), io.start(eq, qv), io.start(low.at[pl.ds(0, width)], lv), io.start(eu, uv)]
    y_read.wait()

    def emit(at, e, a):
        here = pl.ds(at * channels, channels)
        ov[:, here] = lax.dot_general(e, a, TN, preferred_element_type=F32).astype(BF)
        io.put(ov.at[:, here], out.at[:, here])

    for dj in range(3):
        t_reads[dj].wait()
        for di in range(3):
            emit(3 * di + dj, yv[...], tv[dj, di * COLS : di * COLS + width, :])
    wait(*reads)
    emit(TAPS, uv[...], lv[...])
    emit(TAPS + 1, qv[...], pv[...])
    io.finish()


def trunk_result_kernel(tasks, parts, *refs):
    outs = refs[:-1]
    quarter = parts[0].shape[1] // (TAPS * len(outs))
    for k in range(4):
        ref = parts[k]
        there = pl.ds(pl.multiple_of(tasks[k] * quarter, quarter), quarter)
        for layer, out in enumerate(outs):
            for t in range(TAPS):
                start = (layer * TAPS + t) * quarter
                out[t, :, there] = ref[:, start : start + quarter].astype(F32)


def branch_result_kernel(tasks, norm_tasks, parts, norms, out, in_out, mask_out, gains, biases, sems):
    channels = in_out.shape[2]
    for k in range(4):
        ref = parts[k]
        task = tasks[k]

        @pl.when(task < TASKS)
        def _():
            for t in range(TAPS + 2):
                block = ref[:, t * channels : (t + 1) * channels].astype(F32)
                if t < TAPS:
                    out[task, t] = block
                elif t == TAPS:
                    in_out[task] = block
                else:
                    mask_out[task] = block

        @pl.when(norm_tasks[k] < TASKS)
        def _():
            for i in range(3):
                sums = norms[k][i]
                gains[norm_tasks[k], i : i + 1, :] = sums[2:3] + sums[3:4]
                biases[norm_tasks[k], i : i + 1, :] = sums[0:1] + sums[1:2]


VMEM = pl.BlockSpec(memory_space=pltpu.VMEM)
SPARE = 6 * MIB


class Near:
    def __init__(self, value):
        self.value = value


def bytes_of(a):
    return math.prod(a.shape) * jnp.dtype(a.dtype).itemsize


def run(kernel, ins, outs, scratch, flops=0, copies=64, near=False, deps=(), aliases=None):
    flat, specs, groups, resident = [], [], [], 0
    for item in ins:
        parts = list(item) if isinstance(item, (list, tuple)) else [item]
        groups.append(len(parts) if isinstance(item, (list, tuple)) else 0)
        for part in parts:
            kept = near or isinstance(part, Near)
            part = part.value if isinstance(part, Near) else part
            if part.ndim == 1:
                specs.append(SMEM)
            elif kept:
                specs.append(VMEM)
                resident += bytes_of(part)
                if not near:
                    part = pltpu.with_memory_space_constraint(part, pltpu.VMEM)
            else:
                specs.append(HBM)
                part = pltpu.with_memory_space_constraint(part, pltpu.HBM)
            flat.append(part)
    shapes, out_specs = [], []
    for item in outs:
        kept = near or isinstance(item, Near)
        item = item.value if isinstance(item, Near) else item
        if not near:
            item = (pltpu.VMEM if kept else pltpu.HBM)(item.shape, item.dtype)
        shapes.append(item)
        out_specs.append(VMEM if kept else HBM)
        resident += bytes_of(item) if kept else 0
    resident += sum(bytes_of(b) for b in scratch)
    size = sum(bytes_of(a) for a in flat) + sum(bytes_of(o) for o in shapes)
    count = len(flat)

    def body(*refs):
        rest, args = list(refs[:count]), []
        for group in groups:
            if group:
                args.append(tuple(rest[:group]))
                rest = rest[group:]
            else:
                args.append(rest.pop(0))
        kernel(*args, *refs[count + len(deps) :])

    return pl.pallas_call(
        body,
        out_shape=shapes,
        in_specs=specs + [ANY] * len(deps),
        out_specs=out_specs,
        scratch_shapes=list(scratch) + [pltpu.SemaphoreType.DMA((copies,))],
        input_output_aliases=aliases or {},
        compiler_params=pltpu.CompilerParams(vmem_limit_bytes=resident + SPARE),
        cost_estimate=pl.CostEstimate(flops=flops, bytes_accessed=size, transcendentals=0),
    )(*flat, *deps)


def after(value, *others):
    return pl.pallas_call(
        lambda *refs: None,
        out_shape=jax.ShapeDtypeStruct(value.shape, value.dtype),
        in_specs=[HBM] + [ANY] * len(others),
        out_specs=HBM,
        input_output_aliases={0: 0},
    )(value, *others)


def swap(value, axis, mask):
    pairs = [(i, i ^ mask) for i in range(lax.axis_size(axis))]
    return lax.ppermute(value, axis, pairs)


def cross(value, second):
    tasks, width = lax.axis_size("task"), lax.axis_size("dp")
    pairs = []
    for t in range(tasks):
        for d in range(width):
            mask = 1 if (d + second) % 2 == 0 else 2
            pairs.append((t * width + d, (t ^ mask) * width + d))
    return lax.ppermute(value, ("task", "dp"), pairs)


def all_of(value, axis, unit):
    if lax.axis_size(axis) == 4 * unit:
        return [value] + [swap(value, axis, unit * k) for k in (1, 2, 3)]
    mask = unit
    while mask < lax.axis_size(axis):
        value = value + swap(value, axis, mask)
        mask *= 2
    return [value]


def total(parts):
    return (parts[0] + parts[1]) + (parts[2] + parts[3]) if len(parts) == 4 else parts[0]


def sum_parts(pay):
    return all_of(pay + swap(pay, "dp", 1), "dp", 2)


def exchange(pay):
    recv = swap(pay, "dp", 1)
    return recv, all_of(pay[COLS:] + recv[COLS:], "dp", 2)


def join(*parts):
    return jnp.concatenate(parts, axis=0)


def gather_column(part):
    return join(part, swap(part, "dp", 2), swap(part, "dp", 4), swap(part, "dp", 6))


def gather_plane(column):
    first = cross(column, 0)
    return [column, first, cross(column, 1), cross(first, 1)]


def gather_core(parts):
    return parts + [swap(part, "dp", 1) for part in parts]


def domain_counts(size_class, domain_tags):
    big_area = HEIGHT * WIDTH
    small_area = BAND * HALF_WIDTH
    ones_count = jnp.sum(
        jnp.where(
            size_class == 0, big_area * domain_tags[:, 0], small_area * jnp.sum(domain_tags, axis=1)
        )
    )
    all_count = size_class.shape[0] * big_area
    return jnp.maximum(jnp.stack([all_count - ones_count, ones_count]).astype(F32), 1.0)


def on_device(
    images,
    conv_first,
    conv_second,
    conv_third,
    trunk_gains,
    trunk_biases,
    attend_in,
    attend_mask,
    attend_out,
    branch_gains,
    branch_biases,
    size_class,
    domain_tags,
    trunk_cotangent,
    task_cotangent,
):
    rows, cols, ch = images.shape
    pixels = rows * cols
    position = lax.axis_index("dp")
    task_index = lax.axis_index("task")
    width = lax.axis_size("dp")
    task_count = lax.axis_size("task")
    quarter = ch // task_count
    own_out = ch // width
    by_permute = width == 8 and task_count == 4 and own_out == task_count * PIECE
    pair_index = position // 2
    bottom = position % 2
    local_class = lax.dynamic_slice_in_dim(size_class, pair_index * CANVAS, CANVAS, 0)
    local_tags = lax.dynamic_slice_in_dim(domain_tags, pair_index * CANVAS, CANVAS, 0)
    side = jnp.arange(GROUPS) % 2
    slot_class = jnp.repeat(local_class, 2)
    slot_tags = jnp.repeat(local_tags, 2, axis=0)
    which = jnp.where(slot_class == 1, bottom * 2 + side, 0)
    groups = jnp.sum(slot_tags * (jnp.arange(4)[None, :] == which[:, None]), axis=1)
    active = (task_index < TASKS).astype(jnp.int32)
    branch = jnp.minimum(task_index, TASKS - 1)
    info = jnp.concatenate(
        [groups, local_class, jnp.stack([bottom, task_index, active, branch, position])]
    ).astype(jnp.int32)
    cnt = domain_counts(size_class, domain_tags)

    def shape(dims, dtype=F32):
        return jax.ShapeDtypeStruct(dims, dtype)

    z_index, core = position // 2, position % 2
    masks_of = (jnp.where(core == 0, 1, 2), jnp.where(core == 0, 2, 1))
    places = []
    for side_core, (m1, m2) in ((core, masks_of), (1 - core, masks_of[::-1])):
        for t in (task_index, task_index ^ m1, task_index ^ m2, task_index ^ m1 ^ m2):
            for zz in (z_index, z_index ^ 1, z_index ^ 2, z_index ^ 3):
                places.append((2 * zz + side_core) * own_out + t * (own_out // task_count))
    place = jnp.stack(places).astype(jnp.int32)
    pieces_of_task = [task_index, task_index ^ masks_of[0], task_index ^ masks_of[1], task_index ^ 3]
    task_order = jnp.stack(pieces_of_task).astype(jnp.int32)
    norm_order = jnp.stack([task_index ^ k for k in range(4)]).astype(jnp.int32)
    spot = jnp.stack([task_index, branch]).astype(jnp.int32)

    def by_tap(kernel):
        kernel = jnp.swapaxes(kernel, -1, -2)
        tasks = kernel.shape[:1] if kernel.ndim % 2 else ()
        return kernel.reshape(tasks + (-1,) + kernel.shape[-2:])

    def cast(sources, out_rows, pick, deps=()):
        sources = [by_tap(k) for k in sources]
        taps_of = [k.shape[-3] for k in sources]
        (out,) = pl.pallas_call(
            functools.partial(cast_kernel, pick, len(sources)),
            out_shape=[shape((out_rows, sum(taps_of) * ch), BF)],
            in_specs=[SMEM] + [HBM] * len(sources) + [ANY] * len(deps),
            out_specs=[VMEM],
            scratch_shapes=[pltpu.VMEM((n, out_rows, ch), F32) for n in taps_of]
            + [pltpu.SemaphoreType.DMA((len(sources),))],
            compiler_params=pltpu.CompilerParams(vmem_limit_bytes=32 * MIB),
        )(spot, *(pltpu.with_memory_space_constraint(k, pltpu.HBM) for k in sources), *deps)
        return out

    def pick(values):
        return lax.dynamic_index_in_dim(values, branch, 0, keepdims=False)

    params = jnp.concatenate(
        [trunk_gains, pick(branch_gains), trunk_biases, pick(branch_biases), jnp.zeros((4, ch), F32)]
    )
    flat = images.reshape(pixels, ch)
    edge = jnp.where(bottom == 1, flat[:COLS], flat[pixels - COLS :])
    gather = functools.partial(lax.all_gather, axis_name="dp", axis=0, tiled=True)
    halo = swap(edge, "dp", 1)
    early = [params, halo]
    later = []
    if by_permute:
        column_1 = gather_column(cast([conv_first], PIECE, True))
        plane_1 = gather_plane(column_1)
        weights_1 = gather_core(plane_1)
        weights_2 = [gather(cast([conv_second], own_out, False, [column_1]))]
        later = plane_1[1:3]
        column_3 = gather_column(cast([conv_third], PIECE, True, later))
        first, second = cross(column_3, 0), cross(column_3, 1)
        plane_3 = [column_3, first, second, cross(first, 1)]
        weights_3 = gather_core(plane_3)
        early.append(column_3)
    else:
        weights_1, weights_2, weights_3 = [
            [gather(cast([k], own_out, False))] for k in (conv_first, conv_second, conv_third)
        ]
        plane_3 = []
    weights = [weights_1, weights_2, weights_3]
    cast_pair = cast([attend_in, attend_mask], own_out, False, later)
    cast_out = cast([attend_out], own_out, False, later)
    w_pair = gather(cast_pair)
    w_out = gather(cast_out)
    early += [cast_pair, cast_out]

    wide = shape((pixels, ch))
    low_wide = shape((pixels, ch), BF)
    pay_shape = shape((COLS + 8, ch))
    sums_shape = shape((8, ch))
    taps_dims = (3, pixels + 2 * COLS, ch)
    v_params = pltpu.VMEM((16, ch), F32)
    v_wide = pltpu.VMEM((pixels, ch), F32)
    v_low = pltpu.VMEM((pixels, ch), BF)
    v_pay = pltpu.VMEM((COLS + 8, ch), F32)
    v_sums = pltpu.VMEM((8, ch), F32)
    v_four = pltpu.VMEM((4, 8, ch), F32)
    v_pool = pltpu.VMEM((pixels // 4, ch), BF)
    v_conv = pltpu.VMEM((ch, TAPS * ch), BF)
    v_dot = pltpu.VMEM((ch, ch), BF)
    v_quarter = pltpu.VMEM((3, pixels + 2 * COLS, quarter), BF)
    taps = pltpu.VMEM(taps_dims, BF)
    masks = pltpu.VMEM((2, COLS, 128), F32)
    acc = pltpu.VMEM((2, GROUPS, 8, ch), F32)
    buf = pltpu.VMEM((ch // 128, COLS, 128), F32)

    def coefs(blocks):
        return pltpu.VMEM((4 * blocks, ch), F32)

    conv_flops = 2 * TAPS * pixels * ch * ch
    dot_flops = 2 * pixels * ch * ch

    quarter_shape = shape((3, pixels + 2 * COLS, quarter), BF)
    z, recv, stats, quarters = [], [], [], []
    outs = [wide, Near(wide), pay_shape, quarter_shape]
    near = None
    for layer in range(3):
        if layer == 0:
            values, near, pay, part = run(
                functools.partial(first_conv_kernel, rows),
                [info, place, flat, halo, weights_1],
                outs, [v_low, pltpu.VMEM((COLS, ch), BF), v_pay, v_conv, taps, masks, acc], conv_flops,
                deps=early,
            )
        else:
            values, near, pay, part = run(
                functools.partial(conv_kernel, rows, layer - 1),
                [info, cnt, place, params, Near(near), recv[-1], stats[-1], weights[layer]],
                outs, [v_params, v_pay, v_four, v_pay, v_conv, taps, masks, acc, coefs(4)], conv_flops,
                deps=plane_3 if layer == 1 else (),
            )
        got, found = exchange(pay)
        z.append(values)
        recv.append(got)
        stats.append(found)
        quarters.append(part)

    low, trunk_pool, u, near, pay = run(
        functools.partial(enter_kernel, rows, 2),
        [info, cnt, params, Near(near), recv[2], stats[2], w_pair],
        [shape((pixels + COLS, ch), BF), shape((pixels // 4, ch), BF), wide, Near(wide), sums_shape],
        [v_params, v_pay, v_four, v_dot, pltpu.VMEM((pixels + COLS, ch), BF), v_pool, v_sums, acc,
         coefs(4), buf], dot_flops,
    )
    u_stats = sum_parts(pay)
    p, q, near, pay = run(
        functools.partial(mask_kernel, rows, 3),
        [info, cnt, params, Near(near), u_stats, w_pair],
        [low_wide, wide, Near(wide), pay_shape],
        [v_params, v_four, v_dot, v_low, v_pay, acc, coefs(4)], dot_flops,
    )
    q_recv, q_stats = exchange(pay)
    y, near, pay, masked_taps = run(
        functools.partial(branch_conv_kernel, rows, 4),
        [info, cnt, params, low, Near(near), q_recv, q_stats, w_out],
        [wide, Near(wide), pay_shape, shape(taps_dims, BF)],
        [v_params, pltpu.VMEM((pixels + COLS, ch), BF), v_pay, v_four, v_pay, v_conv, taps, masks, acc,
         coefs(4)], conv_flops,
    )
    y_recv, y_stats = exchange(pay)

    branch_pool, near, pay = run(
        functools.partial(turn_kernel, rows, 5),
        [info, cnt, params, Near(near), y_stats, task_cotangent.reshape(TASKS, pixels // 4, ch)],
        [shape((pixels // 4, ch), BF), Near(wide), pay_shape],
        [v_params, v_four, v_pool, v_pool, v_pay, acc, coefs(4), buf],
    )
    task_features = lax.all_gather(branch_pool, "task")
    gy_recv, y_sums = exchange(pay)
    e_y, near, gs, pay = run(
        functools.partial(branch_back_kernel, rows),
        [info, cnt, params, Near(near), y, gy_recv, y_recv, y_stats, y_sums, w_out, low, q, q_stats],
        [low_wide, Near(wide), wide, sums_shape],
        [v_params, v_wide, v_pay, v_pay, v_four, v_four, v_four, v_low, v_wide, v_low, v_sums, v_conv,
         taps, masks, acc, coefs(10)], conv_flops,
    )
    q_sums = sum_parts(pay)
    e_q, near, pay = run(
        functools.partial(mask_back_kernel, rows),
        [info, cnt, params, Near(near), q, q_stats, q_sums, w_pair, u, u_stats],
        [low_wide, Near(wide), sums_shape],
        [v_params, v_wide, v_wide, v_four, v_four, v_four, v_dot, v_low, v_sums, acc, coefs(10)], dot_flops,
    )
    u_sums = sum_parts(pay)
    e_u, grad_shared, pay = run(
        functools.partial(leave_kernel, rows),
        [info, cnt, params, Near(near), u, u_stats, u_sums, w_pair, gs, z[2], stats[2],
         trunk_cotangent.reshape(pixels // 4, ch)],
        [low_wide, low_wide, sums_shape],
        [v_params, v_wide, v_wide, v_four, v_four, v_four, v_dot, v_wide, v_wide, v_pool, v_low, v_low, v_sums, acc,
         coefs(10), buf], dot_flops, deps=[task_features],
    )
    sums = all_of(total(sum_parts(pay)), "task", 1)
    grad_half = grad_shared + after(cross(grad_shared, 0), *sums)
    grad_rest = cross(grad_half, 1)
    (branch_part,) = run(
        functools.partial(branch_wgrad_kernel, rows),
        [masked_taps, e_y, p, e_q, low, e_u],
        [shape((ch, 11 * ch), BF)],
        [taps, v_low, v_low, v_low, v_low, v_low, pltpu.VMEM((ch, 11 * ch), BF)], conv_flops, deps=[grad_half],
    )
    branch_part = after(branch_part, grad_rest)
    branch_part = lax.psum_scatter(branch_part, "dp", scatter_dimension=0, tiled=True)

    edge = jnp.where(
        bottom == 1, grad_half[:COLS] + grad_rest[:COLS], grad_half[-COLS:] + grad_rest[-COLS:]
    )
    g, g_recv = [grad_half, grad_rest], swap(edge, "dp", 1)
    parts = [None, None, None]
    trunk_sums = [None, None, None]
    for layer in (2, 1):
        trunk_sums[layer] = sums
        top = layer == 2
        e, near, pay = run(
            functools.partial(trunk_back_kernel, rows, layer, top),
            [info, cnt, place, params, g, z[layer], g_recv, recv[layer], stats[layer], sums, z[layer - 1],
             stats[layer - 1], weights[layer]],
            [low_wide, Near(wide), pay_shape],
            [v_params, v_wide, pltpu.VMEM((COLS, ch), BF) if top else v_pay, v_pay, v_four, v_four, v_wide, v_four,
             v_low, v_pay, v_conv, taps, masks, coefs(10), acc] + ([v_low, v_low] if top else []), conv_flops,
            deps=parts[2:] if layer == 1 else (),
        )
        (part,) = run(
            functools.partial(trunk_wgrad_kernel, rows),
            [quarters[layer], e], [shape((ch, TAPS * quarter), BF)],
            [v_quarter, v_low, pltpu.VMEM((ch, TAPS * quarter), BF)], conv_flops // 4,
        )
        parts[layer] = part
        g_recv, sums = exchange(pay)
        g = Near(near)
    later_part = lax.psum_scatter(
        jnp.concatenate(parts[1:], axis=1), "dp", scatter_dimension=0, tiled=True
    )
    branch_first, branch_second = cross(branch_part, 0), cross(branch_part, 1)
    branch_third = cross(branch_first, 1)
    trunk_sums[0] = sums
    half_out = shape((ch // 2, TAPS * quarter), BF)
    last_kernel = functools.partial(last_grad_kernel, rows)
    if not by_permute:
        last_kernel = functools.partial(whole_last_grad_kernel, rows)
    e, *halves = run(
        last_kernel,
        [info, place, cnt, params, g, z[0], g_recv, recv[0], stats[0], sums, quarters[0]],
        [shape((pixels + 2 * COLS, ch), BF)]
        + ([half_out, half_out] if by_permute else [shape((ch, TAPS * quarter), BF)]),
        [v_params, v_wide, v_pay, v_pay, v_four, v_four, v_quarter, pltpu.VMEM((pixels + 2 * COLS, ch), BF),
         pltpu.VMEM((ch, TAPS * quarter), BF), coefs(10)], conv_flops // 4,
        deps=[parts[1], branch_first, branch_second],
    )

    def input_grad(m, before, deps):
        tile = TILE_ROWS * COLS
        ins = [info, place, e, weights[0]] + before
        (out,) = run(
            functools.partial(last_conv_kernel, m), ins, [wide],
            [pltpu.VMEM((tile + 2 * COLS, ch), BF), pltpu.VMEM((tile, ch), F32), v_conv,
             pltpu.VMEM((3, tile + 2 * COLS, ch), BF), masks], conv_flops // 3, deps=deps,
            aliases={2 + len(weights[0]) + 1: 0} if before else None,
        )
        return [out]

    def plane(part, *others):
        first, second = cross(part, 0), cross(part, 1)
        return [part, first, second, cross(after(first, *others) if others else first, 1)]

    tiles = rows // TILE_ROWS
    norm_sums = jnp.stack([total(s)[:4] for s in (u_sums, q_sums, y_sums)])
    if by_permute:
        mine, other = halves
        half = mine.shape[0] // 2
        got = swap(other, "dp", 1)
        images_grad = input_grad(0, [], [got])
        send, keep = mine[half:] + got[half:], mine[:half] + got[:half]
        got = swap(send, "dp", 2)
        images_grad = input_grad(1, images_grad, [got])
        later_parts = plane(after(later_part, got))
        half = half // 2
        send, keep = keep[half:] + got[half:], keep[:half] + got[:half]
        norm_sums = after(norm_sums, got)
        got = after(swap(send, "dp", 4), *images_grad)
        first_part = keep + got
        for m in range(2, tiles):
            images_grad = input_grad(m, images_grad, [first_part])
        first_parts = plane(first_part, *images_grad)
        result_deps = [first_parts[1]]
    else:
        first_part = lax.psum_scatter(halves[0], "dp", scatter_dimension=0, tiled=True)
        images_grad, result_deps = [], []
        for m in range(tiles):
            images_grad = input_grad(m, images_grad, [])
        first_parts, later_parts = plane(first_part), plane(later_part)
    (images_grad,) = images_grad
    out_grad, in_grad, mask_grad, branch_gains_grad, branch_biases_grad = run(
        branch_result_kernel,
        [task_order, norm_order, [branch_part, branch_first, branch_second, branch_third],
         [norm_sums] + [swap(norm_sums, "task", k) for k in (1, 2, 3)]],
        [shape((TASKS, TAPS, own_out, ch)), shape((TASKS, own_out, ch)), shape((TASKS, own_out, ch)),
         shape((TASKS, 3, ch)), shape((TASKS, 3, ch))],
        [], near=True, deps=result_deps,
    )
    grad_shape = shape((TAPS, own_out, ch))
    later_grads = run(
        trunk_result_kernel, [task_order, later_parts], [grad_shape] * 2, [], near=True, deps=result_deps
    )
    (first_grad,) = run(trunk_result_kernel, [task_order, first_parts], [grad_shape], [], near=True)
    kernel_grads = [
        jnp.swapaxes(k.reshape(3, 3, own_out, ch), 2, 3) for k in (first_grad, *later_grads)
    ]
    trunk_sums = jnp.stack([total(s)[:4] for s in trunk_sums])
    return (
        trunk_pool.reshape(rows // 2, cols // 2, ch),
        task_features[:TASKS].reshape(TASKS, rows // 2, cols // 2, ch),
        images_grad.reshape(rows, cols, ch),
        *kernel_grads,
        trunk_sums[:, 2] + trunk_sums[:, 3],
        trunk_sums[:, 0] + trunk_sums[:, 1],
        jnp.swapaxes(in_grad, 1, 2),
        jnp.swapaxes(mask_grad, 1, 2),
        jnp.swapaxes(out_grad.reshape(TASKS, 3, 3, own_out, ch), 3, 4),
        branch_gains_grad,
        branch_biases_grad,
    )


def solution(mesh):
    in_specs = (
        P("dp", None, None),
        P(None, None, None, "dp"),
        P(None, None, None, "dp"),
        P(None, None, None, "dp"),
        P(),
        P(),
        P(None, None, "dp"),
        P(None, None, "dp"),
        P(None, None, None, None, "dp"),
        P(),
        P(),
        P(),
        P(),
        P("dp", None, None),
        P(None, "dp", None, None),
    )
    out_specs = (
        P("dp", None, None),
        P(None, "dp", None, None),
        P("dp", None, None),
        P(None, None, None, "dp"),
        P(None, None, None, "dp"),
        P(None, None, None, "dp"),
        P(),
        P(),
        P(None, None, "dp"),
        P(None, None, "dp"),
        P(None, None, None, None, "dp"),
        P(),
        P(),
    )
    return jax.shard_map(
        on_device, mesh=mesh, in_specs=in_specs, out_specs=out_specs, check_vma=False
    )
```

```python
import functools
import math

import jax
import jax.numpy as jnp
from jax import lax
from jax.experimental import pallas as pl
from jax.experimental.pallas import tpu as pltpu
from jax.sharding import PartitionSpec as P

HEIGHT = 36
WIDTH = 48
BAND = 18
HALF_WIDTH = 24
CANVAS = 2
TASKS = 3
COLS = CANVAS * WIDTH
GROUPS = COLS // HALF_WIDTH
EPSILON = 1e-05
TAPS = 9
TILE_ROWS = 6
LANES = 128
PIECE = 16
MIB = 2**20
BF = jnp.bfloat16
F32 = jnp.float32
NT = (((1,), (1,)), ((), ()))
TN = (((0,), (0,)), ((), ()))

ANY = pl.BlockSpec(memory_space=pl.ANY)
HBM = pl.BlockSpec(memory_space=pltpu.HBM)
SMEM = pl.BlockSpec(memory_space=pltpu.SMEM)


def affine(row, co, scale, shift):
    step = row.shape[0] // GROUPS
    return jnp.concatenate(
        [
            row[step * j : step * (j + 1)] * co[4 * scale + j : 4 * scale + j + 1, :]
            + co[4 * shift + j : 4 * shift + j + 1, :]
            for j in range(GROUPS)
        ],
        axis=0,
    )


def scaled(row, co, scale):
    step = row.shape[0] // GROUPS
    return jnp.concatenate(
        [
            row[step * j : step * (j + 1)] * co[4 * scale + j : 4 * scale + j + 1, :]
            for j in range(GROUPS)
        ],
        axis=0,
    )


def sigmoid(v):
    return 0.5 * jnp.tanh(0.5 * v) + 0.5


def silu(v):
    return v * sigmoid(v)


def silu_slope(v):
    s = sigmoid(v)
    return s * (1.0 + v * (1.0 - s))


def norm_coefs(co, base, stats, params, which, cnt, info):
    gain = params[which : which + 1, :]
    bias = params[which + 6 : which + 7, :]
    means, scales = [], []
    for d in range(2):
        mean = stats[d : d + 1, :] / cnt[d]
        var = stats[2 + d : 3 + d, :] / cnt[d] - mean * mean
        means.append(mean)
        scales.append(lax.rsqrt(var + EPSILON))
    for j in range(GROUPS):
        one = info[j] == 1
        mean = jnp.where(one, means[1], means[0])
        scale = jnp.where(one, scales[1], scales[0])
        full = scale * gain
        co[4 * base + j : 4 * base + j + 1, :] = full
        co[4 * base + 4 + j : 4 * base + 5 + j, :] = bias - mean * full
        co[4 * base + 8 + j : 4 * base + 9 + j, :] = scale
        co[4 * base + 12 + j : 4 * base + 13 + j, :] = -mean * scale


def grad_coefs(co, base, norm, sums, cnt, info):
    for j in range(GROUPS):
        one = info[j] == 1
        count = jnp.where(one, cnt[1], cnt[0])
        plain = jnp.where(one, sums[1:2, :], sums[0:1, :]) / count
        cross = jnp.where(one, sums[3:4, :], sums[2:3, :]) / count
        full = co[4 * norm + j : 4 * norm + j + 1, :]
        scale = co[4 * norm + 8 + j : 4 * norm + 9 + j, :]
        shift = co[4 * norm + 12 + j : 4 * norm + 13 + j, :]
        co[4 * base + j : 4 * base + j + 1, :] = -full * cross * scale
        co[4 * base + 4 + j : 4 * base + 5 + j, :] = -full * (plain + cross * shift)


def grad_row(g, z, co, norm, base):
    return scaled(g, co, norm) + affine(z, co, base, base + 1)


def add_sums(acc, slot, values):
    step = HALF_WIDTH // 8
    count = values.shape[0] // COLS
    channels = values.shape[1]
    acc[slot] += jnp.sum(
        values.reshape(count, GROUPS, step, 8, channels), axis=(0, 2)
    )


def put_sums(acc, info, out, start):
    for slot in range(2):
        groups = [jnp.sum(acc[slot, j], axis=0, keepdims=True) for j in range(GROUPS)]
        for d in range(2):
            total = jnp.zeros_like(groups[0])
            for j in range(GROUPS):
                total = total + jnp.where(info[j] == d, groups[j], 0.0)
            row = start + 2 * slot + d
            out[row : row + 1, :] = total
    out[start + 4 : start + 8, :] = jnp.zeros((4, out.shape[1]), F32)


def put_edge(out, ref, info, rows):
    start = jnp.where(info[6] == 1, 0, (rows - 1) * COLS)
    out[0:COLS, :] = ref[pl.ds(pl.multiple_of(start, COLS), COLS), :].astype(out.dtype)


def make_masks(mk, info):
    col = lax.broadcasted_iota(jnp.int32, mk.shape[1:], 0)
    small = (info[4] == 1, info[5] == 1)
    left = (col == 0) | (col == WIDTH)
    right = (col == WIDTH - 1) | (col == COLS - 1)
    for s in range(2):
        left = left | ((col == s * WIDTH + HALF_WIDTH) & small[s])
        right = right | ((col == s * WIDTH + HALF_WIDTH - 1) & small[s])
    mk[0] = jnp.where(left, 0.0, 1.0)
    mk[1] = jnp.where(right, 0.0, 1.0)


def part(ref, c):
    return ref.at[(slice(None),) * (len(ref.shape) - 1) + (pl.ds(c * LANES, LANES),)]


def put_row(taps, at, row, mk):
    here = pl.ds(pl.multiple_of(at * COLS, COLS), COLS)
    taps[0, here, :] = (pltpu.roll(row, 1, 0) * mk[0]).astype(BF)
    taps[1, here, :] = row.astype(BF)
    taps[2, here, :] = (pltpu.roll(row, COLS - 1, 0) * mk[1]).astype(BF)


def keep_large(row, info):
    step = COLS // GROUPS
    keep = [jnp.where(info[4 + j // 2] == 1, 0.0, 1.0) for j in range(GROUPS)]
    return jnp.concatenate(
        [row[step * j : step * (j + 1)] * keep[j] for j in range(GROUPS)], axis=0
    )


def put_halo(taps, make, mk, info, rows):
    for c in range(taps.shape[2] // LANES):
        row = keep_large(make(c), info)
        put_row(part(taps, c), jnp.where(info[6] == 1, 0, rows + 1), row, mk)
        put_row(part(taps, c), jnp.where(info[6] == 1, rows + 1, 0), jnp.zeros_like(row), mk)


def conv_tile(taps, w, at, rows, transpose):
    acc = None
    channels = taps.shape[2]
    for t in range(TAPS):
        di, dj = divmod(t, 3)
        a = taps[dj, (at + di) * COLS : (at + di + rows) * COLS, :]
        if transpose:
            k = w[:, (8 - t) * channels : (9 - t) * channels]
            r = jnp.dot(a, k, preferred_element_type=F32)
        else:
            k = w[:, t * channels : (t + 1) * channels]
            r = lax.dot_general(a, k, NT, preferred_element_type=F32)
        acc = r if acc is None else acc + r
    return acc


def row_at(r):
    return pl.ds(pl.multiple_of(r * COLS, COLS), COLS)


def tile_at(m):
    return slice(m * TILE_ROWS * COLS, (m + 1) * TILE_ROWS * COLS)


def loop(count, body):
    def step(i, carry):
        body(i)
        return carry

    lax.fori_loop(0, count, step, 0)


def pooled(buf, values):
    half = COLS // 2
    buf[...] = values
    return (buf[pl.ds(0, half, stride=2), :] + buf[pl.ds(1, half, stride=2), :]) * 0.25


def spread(buf, values):
    half = COLS // 2
    quarter = values.astype(F32) * 0.25
    buf[pl.ds(0, half, stride=2), :] = quarter
    buf[pl.ds(1, half, stride=2), :] = quarter
    return buf[...]


class Copies:
    def __init__(self, sems):
        self.sems = sems
        self.used = 0
        self.open = []

    def start(self, src, dst):
        copy = pltpu.make_async_copy(src, dst, self.sems.at[self.used])
        self.used += 1
        copy.start()
        return copy

    def put(self, src, dst):
        self.open.append(self.start(src, dst))

    def tiles(self, src, dst, rows):
        return [
            self.start(src.at[pl.ds(m * TILE_ROWS * COLS, TILE_ROWS * COLS)],
                       dst.at[pl.ds(m * TILE_ROWS * COLS, TILE_ROWS * COLS)])
            for m in range(rows // TILE_ROWS)
        ]

    def put_tile(self, src, dst, m):
        here = pl.ds(m * TILE_ROWS * COLS, TILE_ROWS * COLS)
        self.put(src.at[here], dst.at[here])

    def weights(self, pieces, place, dst):
        if len(pieces) == 1:
            return [self.start(pieces[0], dst)]
        copies = []
        count = pieces[0].shape[0] // PIECE
        for i, piece in enumerate(pieces):
            for k in range(count):
                row = pl.multiple_of(place[i * count + k], PIECE)
                copies.append(
                    self.start(piece.at[pl.ds(k * PIECE, PIECE)], dst.at[pl.ds(row, PIECE)])
                )
        return copies

    def finish(self):
        for copy in self.open:
            copy.wait()


def bring(io, ref, rest, count, rows):
    if len(rest) == count:
        return ref, [()] * (rows // TILE_ROWS), rest
    return rest[0], [(copy,) for copy in io.tiles(ref, rest[0], rows)], rest[1:]


def put_norms(norms, i, sums):
    norms[i : i + 1, :] = sums[2:3, :] + sums[3:4, :]
    norms[3 + i : 4 + i, :] = sums[0:1, :] + sums[1:2, :]


def settle(parts, dst):
    if len(parts) == 4:
        dst[...] = (parts[0][...] + parts[1][...]) + (parts[2][...] + parts[3][...])
    else:
        dst[...] = parts[0][...]
    return dst


def wait(*copies):
    for copy in copies:
        copy.wait()


def all_parts(channels, body):
    for c in range(channels // LANES):
        body(c)


def each_pair(m, channels, body):
    half = TILE_ROWS // 2
    loop(half, lambda i: all_parts(channels, lambda c: body(m * half + i, c)))


def each_row(m, channels, body):
    loop(TILE_ROWS, lambda r: all_parts(channels, lambda c: body(m * TILE_ROWS + r, c)))


def cast_kernel(pick, count, spot, *refs):
    sources, out, wide, sems = refs[:count], refs[-count - 2], refs[-count - 1 : -1], refs[-1]
    io = Copies(sems)
    rows, channels = out.shape[0], wide[0].shape[2]
    first = pl.multiple_of(spot[0] * rows, rows) if pick else 0
    reads = []
    for src, dst in zip(sources, wide):
        if len(src.shape) == 4:
            src = src.at[spot[1]]
        reads.append(io.start(src.at[:, pl.ds(first, rows), :], dst))
    start = 0
    for src, read in zip(wide, reads):
        read.wait()
        for t in range(src.shape[0]):
            out[:, start : start + channels] = src[t].astype(BF)
            start += channels


def conv_outputs(rows, info, w, z, zv, pay, quarter, taps, acc, io, w_reads):
    if quarter is not None:
        width = quarter.shape[2]
        io.put(taps.at[:, :, pl.ds(pl.multiple_of(info[7] * width, 128), width)], quarter)
    wait(*w_reads)
    for m in range(rows // TILE_ROWS):
        out = conv_tile(taps, w, m * TILE_ROWS, TILE_ROWS, False)
        zv[tile_at(m), :] = out
        io.put_tile(zv, z, m)
        add_sums(acc, 0, out)
        add_sums(acc, 1, out * out)
    put_edge(pay, zv, info, rows)
    put_sums(acc, info, pay, COLS)


def first_conv_kernel(rows, info, place, x, halo, pieces, z, zv, pay, quarter, xv, wv, taps, mk, acc, sems):
    io = Copies(sems)
    ch = x.shape[1]
    reads = io.tiles(x, xv, rows)
    w_reads = io.weights(pieces, place, wv)
    make_masks(mk, info)
    acc[...] = jnp.zeros_like(acc)
    for m, read in enumerate(reads):
        read.wait()
        each_row(
            m, ch, lambda r, c: put_row(part(taps, c), r + 1, part(xv, c)[row_at(r), :].astype(F32), mk)
        )
    put_halo(taps, lambda c: part(halo, c)[...].astype(F32), mk, info, rows)
    conv_outputs(rows, info, wv, z, zv, pay, quarter, taps, acc, io, w_reads)
    io.finish()


def conv_kernel(
    rows, which, info, cnt, place, params, x, recv, stats, pieces, z, zv, pay, quarter, kept, *rest
):
    io = Copies(rest[-1])
    x, reads, rest = bring(io, x, rest, 7, rows)
    sv, wv, taps, mk, acc, co, _ = rest
    w_reads = io.weights(pieces, place, wv)
    make_masks(mk, info)
    acc[...] = jnp.zeros_like(acc)
    norm_coefs(co, 0, settle(stats, sv), params, which, cnt, info)
    io.put(sv, kept)

    def act(ref, here, c):
        return silu(affine(part(ref, c)[here, :], part(co, c), 0, 1))

    for m, read in enumerate(reads):
        wait(*read)
        each_row(m, x.shape[1], lambda r, c: put_row(part(taps, c), r + 1, act(x, row_at(r), c), mk))
    put_halo(taps, lambda c: act(recv, slice(0, COLS), c), mk, info, rows)
    conv_outputs(rows, info, wv, z, zv, pay, quarter, taps, acc, io, w_reads)
    io.finish()


def enter_kernel(
    rows, which, info, cnt, params, x, recv, stats, w, low, pool, u, uv, pay, kept, *rest
):
    io = Copies(rest[-1])
    x, reads, rest = bring(io, x, rest, 8, rows)
    sv, wv, lowv, poolv, acc, co, buf, _ = rest
    w_read = io.start(w.at[:, pl.ds(0, wv.shape[1])], wv)
    acc[...] = jnp.zeros_like(acc)
    norm_coefs(co, 0, settle(stats, sv), params, which, cnt, info)
    io.put(sv, kept)
    half = COLS // 2
    ch = x.shape[1]

    def act(ref, here, c):
        return silu(affine(part(ref, c)[here, :], part(co, c), 0, 1))

    def pair(i, c):
        first, second = act(x, row_at(2 * i), c), act(x, row_at(2 * i + 1), c)
        part(lowv, c)[row_at(2 * i), :] = first.astype(BF)
        part(lowv, c)[row_at(2 * i + 1), :] = second.astype(BF)
        part(poolv, c)[pl.ds(pl.multiple_of(i * half, half), half), :] = pooled(
            buf.at[c], first + second
        ).astype(BF)

    for c in range(ch // LANES):
        part(lowv, c)[rows * COLS : (rows + 1) * COLS, :] = act(recv, slice(0, COLS), c).astype(BF)
    for m, read in enumerate(reads):
        wait(*read)
        each_pair(m, ch, pair)
        if m == 0:
            w_read.wait()
        out = lax.dot_general(lowv[tile_at(m), :], wv[...], NT, preferred_element_type=F32)
        uv[tile_at(m), :] = out
        io.put_tile(uv, u, m)
        add_sums(acc, 0, out)
        add_sums(acc, 1, out * out)
    io.put(lowv, low)
    io.put(poolv, pool)
    put_sums(acc, info, pay, 0)
    io.finish()


def mask_kernel(
    rows, which, info, cnt, params, u, stats, w, p, q, qv, pay, kept, sv, wv, ev, acc, co, sems
):
    io = Copies(sems)
    w_read = io.start(w.at[:, pl.ds(wv.shape[1], wv.shape[1])], wv)
    acc[...] = jnp.zeros_like(acc)
    norm_coefs(co, 0, settle(stats, sv), params, which, cnt, info)
    io.put(sv, kept)

    def each(r, c):
        part(ev, c)[row_at(r), :] = silu(affine(part(u, c)[row_at(r), :], part(co, c), 0, 1)).astype(BF)

    for m in range(rows // TILE_ROWS):
        each_row(m, u.shape[1], each)
        io.put_tile(ev, p, m)
        if m == 0:
            w_read.wait()
        out = lax.dot_general(ev[tile_at(m), :], wv[...], NT, preferred_element_type=F32)
        qv[tile_at(m), :] = out
        io.put_tile(qv, q, m)
        add_sums(acc, 0, out)
        add_sums(acc, 1, out * out)
    put_edge(pay, qv, info, rows)
    put_sums(acc, info, pay, COLS)
    io.finish()


def branch_conv_kernel(
    rows, which, info, cnt, params, low, q, recv, stats, w, y, yv, pay, wide_taps, kept, *rest
):
    io = Copies(rest[-1])
    q, reads, rest = bring(io, q, rest, 8, rows)
    lv, sv, wv, taps, mk, acc, co, _ = rest
    low_read = io.start(low, lv)
    w_read = io.start(w, wv)
    make_masks(mk, info)
    acc[...] = jnp.zeros_like(acc)
    norm_coefs(co, 0, settle(stats, sv), params, which, cnt, info)
    io.put(sv, kept)

    def masked(at, ref, here, c):
        gate = sigmoid(affine(part(ref, c)[here, :], part(co, c), 0, 1))
        return part(lv, c)[at, :].astype(F32) * gate

    low_read.wait()
    for m, read in enumerate(reads):
        wait(*read)
        each_row(
            m, q.shape[1],
            lambda r, c: put_row(part(taps, c), r + 1, masked(row_at(r), q, row_at(r), c), mk),
        )
    put_halo(
        taps, lambda c: masked(slice(rows * COLS, (rows + 1) * COLS), recv, slice(0, COLS), c), mk, info, rows
    )
    io.put(taps, wide_taps)
    conv_outputs(rows, info, wv, y, yv, pay, None, taps, acc, io, [w_read])
    io.finish()


def turn_kernel(
    rows, which, info, cnt, params, y, stats, cot, pool, g, pay, kept, gv, sv, cv, poolv, acc, co, buf, sems
):
    io = Copies(sems)
    cot_read = io.start(cot.at[info[9]], cv)
    acc[...] = jnp.zeros_like(acc)
    norm_coefs(co, 0, settle(stats, sv), params, which, cnt, info)
    io.put(sv, kept)
    half = COLS // 2

    def pair(i, c):
        here = pl.ds(pl.multiple_of(i * half, half), half)
        ct = spread(buf.at[c], part(cv, c)[here, :])
        total = None
        for k in range(2):
            at = row_at(2 * i + k)
            row = part(y, c)[at, :]
            v = affine(row, part(co, c), 0, 1)
            s = sigmoid(v)
            f = v * s
            total = f if total is None else total + f
            gr = ct * (s * (1.0 + v * (1.0 - s)))
            part(gv, c)[at, :] = gr
            add_sums(part(acc, c), 0, gr)
            add_sums(part(acc, c), 1, gr * affine(row, part(co, c), 2, 3))
        part(poolv, c)[here, :] = pooled(buf.at[c], total).astype(BF)

    cot_read.wait()
    for m in range(rows // TILE_ROWS):
        each_pair(m, y.shape[1], pair)
        io.put_tile(gv, g, m)
    io.put(poolv, pool)
    put_edge(pay, gv, info, rows)
    put_sums(acc, info, pay, COLS)
    io.finish()


def branch_back_kernel(
    rows, info, cnt, params, g, y, recv_g, recv_y, stats, sums, w, low, q, qstats,
    e, gv, gs, pay, norms, gin, yv, hv, sv, tv, qsv, lv, qv, ev, wv, taps, mk, acc, co, sems,
):
    io = Copies(sems)
    small = [io.start(stats, sv), io.start(qstats, qsv), io.start(recv_y, hv)]
    reads = list(zip(io.tiles(g, gin, rows), io.tiles(y, yv, rows)))
    w_read = io.start(w, wv)
    low_read = io.start(low.at[pl.ds(0, rows * COLS)], lv)
    q_read = io.start(q, qv)
    make_masks(mk, info)
    acc[...] = jnp.zeros_like(acc)
    wait(*small)
    norm_coefs(co, 0, sv, params, 5, cnt, info)
    grad_coefs(co, 4, 0, settle(sums, tv), cnt, info)
    norm_coefs(co, 6, qsv, params, 4, cnt, info)
    norms[...] = jnp.zeros_like(norms)
    put_norms(norms, 2, tv)

    ch = gv.shape[1]

    def grad(g_ref, y_ref, here, c):
        return grad_row(part(g_ref, c)[here, :], part(y_ref, c)[here, :], part(co, c), 0, 4)

    def each(r, c):
        row = grad(gin, yv, row_at(r), c)
        part(ev, c)[row_at(r), :] = row.astype(BF)
        put_row(part(taps, c), r + 1, row, mk)

    for m, pair in enumerate(reads):
        wait(*pair)
        each_row(m, ch, each)
        io.put_tile(ev, e, m)
    put_halo(taps, lambda c: grad(recv_g, hv, slice(0, COLS), c), mk, info, rows)
    wait(w_read, low_read, q_read)

    def post(r, c):
        here = row_at(r)
        value = part(gv, c)[here, :]
        row = part(qv, c)[here, :]
        gate = sigmoid(affine(row, part(co, c), 6, 7))
        value = value * gate
        part(yv, c)[here, :] = value
        out = value * part(lv, c)[here, :].astype(F32) * (1.0 - gate)
        part(gv, c)[here, :] = out
        add_sums(part(acc, c), 0, out)
        add_sums(part(acc, c), 1, out * affine(row, part(co, c), 8, 9))

    for m in range(rows // TILE_ROWS):
        gv[tile_at(m), :] = conv_tile(taps, wv, m * TILE_ROWS, TILE_ROWS, True)
        each_row(m, ch, post)
        io.put_tile(yv, gs, m)
    put_sums(acc, info, pay, 0)
    io.finish()


def mask_back_kernel(
    rows, info, cnt, params, g, q, stats, sums, w, u, ustats, before, e, gv, pay, norms,
    qv, uv, sv, tv, usv, wv, ev, acc, co, sems,
):
    io = Copies(sems)
    small = [io.start(stats, sv), io.start(ustats, usv)]
    reads = io.tiles(q, qv, rows)
    w_read = io.start(w.at[:, pl.ds(wv.shape[1], wv.shape[1])], wv)
    u_reads = io.tiles(u, uv, rows)
    acc[...] = jnp.zeros_like(acc)
    wait(*small)
    norm_coefs(co, 0, sv, params, 4, cnt, info)
    grad_coefs(co, 4, 0, settle(sums, tv), cnt, info)
    norm_coefs(co, 6, usv, params, 3, cnt, info)
    norms[...] = before[...]
    put_norms(norms, 1, tv)

    ch = g.shape[1]

    def each(r, c):
        here = row_at(r)
        part(ev, c)[here, :] = grad_row(
            part(g, c)[here, :], part(qv, c)[here, :], part(co, c), 0, 4
        ).astype(BF)

    def post(r, c):
        here = row_at(r)
        row = part(uv, c)[here, :]
        out = part(gv, c)[here, :] * silu_slope(affine(row, part(co, c), 6, 7))
        part(gv, c)[here, :] = out
        add_sums(part(acc, c), 0, out)
        add_sums(part(acc, c), 1, out * affine(row, part(co, c), 8, 9))

    for m, read in enumerate(reads):
        read.wait()
        each_row(m, ch, each)
        io.put_tile(ev, e, m)
        if m == 0:
            w_read.wait()
        gv[tile_at(m), :] = jnp.dot(ev[tile_at(m), :], wv[...], preferred_element_type=F32)
        u_reads[m].wait()
        each_row(m, ch, post)
    put_sums(acc, info, pay, 0)
    io.finish()


def leave_kernel(
    rows, info, cnt, params, g, u, stats, sums, w, gs, z, zstats, cot, before, e, out, pay, norms,
    gv, uv, sv, tv, zsv, wv, gsv, zv, cv, ev, ov, acc, co, buf, sems,
):
    io = Copies(sems)
    small = [io.start(stats, sv), io.start(zstats, zsv)]
    reads = io.tiles(u, uv, rows)
    w_read = io.start(w.at[:, pl.ds(0, wv.shape[1])], wv)
    later = list(zip(io.tiles(gs, gsv, rows), io.tiles(z, zv, rows)))
    cot_read = io.start(cot, cv)
    acc[...] = jnp.zeros_like(acc)
    wait(*small)
    norm_coefs(co, 0, sv, params, 3, cnt, info)
    grad_coefs(co, 4, 0, settle(sums, tv), cnt, info)
    norm_coefs(co, 6, zsv, params, 2, cnt, info)
    norms[...] = before[...]
    put_norms(norms, 0, tv)
    half = COLS // 2
    active = info[8] == 1

    ch = g.shape[1]

    def each(r, c):
        here = row_at(r)
        part(ev, c)[here, :] = grad_row(
            part(g, c)[here, :], part(uv, c)[here, :], part(co, c), 0, 4
        ).astype(BF)

    def post(i, c):
        ct = spread(buf.at[c], part(cv, c)[pl.ds(pl.multiple_of(i * half, half), half), :])
        for k in range(2):
            here = row_at(2 * i + k)
            grad = jnp.where(active, part(gv, c)[here, :] + part(gsv, c)[here, :], ct)
            part(ov, c)[here, :] = grad.astype(BF)
            row = part(zv, c)[here, :]
            grad = grad * silu_slope(affine(row, part(co, c), 6, 7))
            add_sums(part(acc, c), 0, grad)
            add_sums(part(acc, c), 1, grad * affine(row, part(co, c), 8, 9))

    for m, read in enumerate(reads):
        read.wait()
        each_row(m, ch, each)
        io.put_tile(ev, e, m)
        if m == 0:
            wait(w_read, cot_read)
        gv[tile_at(m), :] = jnp.dot(ev[tile_at(m), :], wv[...], preferred_element_type=F32)
        wait(*later[m])
        each_pair(m, ch, post)
        io.put_tile(ov, out, m)
    put_sums(acc, info, pay, 0)
    io.finish()


def trunk_back_kernel(
    rows, which, top, info, cnt, place, params, g, z, recv_g, recv_z, stats, sums, x, xstats, before, pieces,
    e, far, pay, norms, out, zv, kv, sv, tv, xv, xsv, ev, wv, taps, mk, co, acc, *rest
):
    io = Copies(rest[-1])
    small = [io.start(stats, sv), io.start(xstats, xsv), io.start(recv_z, kv)]
    gv = rest[:-1]
    reads = list(zip(*[io.tiles(a, b, rows) for a, b in zip((*g, z), (*gv, zv))]))
    w_reads = io.weights(pieces, place, wv)
    x_reads = io.tiles(x, xv, rows)
    acc[...] = jnp.zeros_like(acc)
    make_masks(mk, info)
    wait(*small)
    norm_coefs(co, 0, sv, params, which, cnt, info)
    grad_coefs(co, 4, 0, settle(sums, tv), cnt, info)
    norm_coefs(co, 6, xsv, params, which - 1, cnt, info)
    norms[...] = before[...]
    put_norms(norms, which, tv)

    ch = z.shape[1]

    def grad(g_refs, z_ref, here, c):
        g_row = part(g_refs[0], c)[here, :].astype(F32)
        for ref in g_refs[1:]:
            g_row = g_row + part(ref, c)[here, :].astype(F32)
        z_row = part(z_ref, c)[here, :]
        if top:
            g_row = g_row * silu_slope(affine(z_row, part(co, c), 0, 1))
        return grad_row(g_row, z_row, part(co, c), 0, 4)

    def each(r, c):
        row = grad(gv, zv, row_at(r), c)
        part(ev, c)[row_at(r), :] = row.astype(BF)
        put_row(part(taps, c), r + 1, row, mk)

    for m, pair in enumerate(reads):
        wait(*pair)
        each_row(m, ch, each)
        io.put_tile(ev, e, m)
    put_halo(taps, lambda c: grad((recv_g,), kv, slice(0, COLS), c), mk, info, rows)
    wait(*w_reads)

    def post(r, c):
        here = row_at(r)
        row = part(xv, c)[here, :]
        value = part(out, c)[here, :] * silu_slope(affine(row, part(co, c), 6, 7))
        part(out, c)[here, :] = value
        add_sums(part(acc, c), 0, value)
        add_sums(part(acc, c), 1, value * affine(row, part(co, c), 8, 9))

    for m in range(rows // TILE_ROWS):
        out[tile_at(m), :] = conv_tile(taps, wv, m * TILE_ROWS, TILE_ROWS, True)
        x_reads[m].wait()
        each_row(m, ch, post)
        io.put_tile(out, far, m)
    put_edge(pay, out, info, rows)
    put_sums(acc, info, pay, COLS)
    io.finish()


def wide_quarter(rows, quarter):
    width = rows * COLS
    return jnp.concatenate(
        [quarter[t % 3, (t // 3) * COLS : (t // 3) * COLS + width, :] for t in range(TAPS)], axis=1
    )


def last_grad_kernel(
    rows, info, place, cnt, params, g, z, recv_g, recv_z, stats, sums, quarter, before,
    e, gains, biases, mine, other, *rest
):
    io = Copies(rest[-1])
    g, g_reads, rest = bring(io, g, rest, 9, rows)
    zv, kv, sv, tv, av, ev, wv, co, _ = rest
    small = [io.start(stats, sv), io.start(recv_z, kv)]
    reads = io.tiles(z, zv, rows)
    a_read = io.start(quarter, av)
    wait(*small)
    norm_coefs(co, 0, sv, params, 0, cnt, info)
    grad_coefs(co, 4, 0, settle(sums, tv), cnt, info)
    gains[0:1, :] = tv[2:3, :] + tv[3:4, :]
    biases[0:1, :] = tv[0:1, :] + tv[1:2, :]
    gains[1:3, :] = before[1:3, :]
    biases[1:3, :] = before[4:6, :]

    def grad(g_ref, z_ref, here, c):
        return grad_row(part(g_ref, c)[here, :], part(z_ref, c)[here, :], part(co, c), 0, 4)

    def each(r, c):
        part(ev, c)[row_at(r + 1), :] = grad(g, zv, row_at(r), c).astype(BF)

    for m, read in enumerate(reads):
        wait(read, *g_reads[m])
        each_row(m, g.shape[1], each)
    for c in range(g.shape[1] // LANES):
        row = keep_large(grad(recv_g, kv, slice(0, COLS), c), info).astype(BF)
        part(ev, c)[row_at(jnp.where(info[6] == 1, 0, rows + 1)), :] = row
        part(ev, c)[row_at(jnp.where(info[6] == 1, rows + 1, 0)), :] = jnp.zeros_like(row)
    io.put(ev, e)
    a_read.wait()
    wv[...] = lax.dot_general(
        ev[COLS : (rows + 1) * COLS, :], wide_quarter(rows, av), TN, preferred_element_type=F32
    ).astype(BF)
    if other is None:
        io.put(wv, mine)
    else:
        size = mine.shape[0] // 4
        for k, mask in enumerate((0, 2, 1, 3)):
            for side, dst in ((0, mine), (1, other)):
                block = info[10] ^ (2 * mask + side)
                src = wv.at[pl.ds(pl.multiple_of(block * size, size), size)]
                io.put(src, dst.at[pl.ds(k * size, size)])
    io.finish()


def whole_last_grad_kernel(rows, *refs):
    last_grad_kernel(rows, *refs[:16], None, *refs[16:])


def last_conv_kernel(m, high, info, place, e, pieces, *refs):
    out, ev, ov, wv, taps, mk, sems = refs[-7:]
    io = Copies(sems)
    read = io.start(e.at[pl.ds(m * high * COLS, (high + 2) * COLS)], ev)
    w_reads = io.weights(pieces, place, wv)
    make_masks(mk, info)
    read.wait()
    loop(
        high + 2,
        lambda r: all_parts(
            ev.shape[1], lambda c: put_row(part(taps, c), r, part(ev, c)[row_at(r), :].astype(F32), mk)
        ),
    )
    wait(*w_reads)
    step = high // 3
    for k in range(3):
        here = pl.ds(k * step * COLS, step * COLS)
        ov[here, :] = conv_tile(taps, wv, k * step, step, True)
        io.put(ov.at[here], out.at[pl.ds((m * high + k * step) * COLS, step * COLS)])
    io.finish()


def trunk_wgrad_kernel(rows, place, quarter, e, *rest):
    parts, av, ev, ov, sems = rest[-5:]
    io = Copies(sems)
    reads = [io.start(quarter, av), io.start(e, ev)]
    wait(*reads)
    ov[...] = lax.dot_general(ev[...], wide_quarter(rows, av), TN, preferred_element_type=F32).astype(BF)
    width = ov.shape[1]
    io.put(ov, parts.at[:, pl.ds(place * width, width)])
    io.finish()


def branch_wgrad_kernel(rows, taps, ey, p, eq, low, eu, out, tv, yv, pv, qv, lv, uv, ov, sems):
    width = rows * COLS
    channels = ey.shape[1]
    io = Copies(sems)
    y_read = io.start(ey, yv)
    t_reads = [io.start(taps.at[k], tv.at[k]) for k in range(3)]
    reads = [io.start(p, pv), io.start(eq, qv), io.start(low.at[pl.ds(0, width)], lv), io.start(eu, uv)]
    y_read.wait()

    def emit(at, e, a):
        here = pl.ds(at * channels, channels)
        ov[:, here] = lax.dot_general(e, a, TN, preferred_element_type=F32).astype(BF)
        io.put(ov.at[:, here], out.at[:, here])

    for dj in range(3):
        t_reads[dj].wait()
        for di in range(3):
            emit(3 * di + dj, yv[...], tv[dj, di * COLS : di * COLS + width, :])
    wait(*reads)
    emit(TAPS, uv[...], lv[...])
    emit(TAPS + 1, qv[...], pv[...])
    io.finish()


def trunk_result_kernel(tasks, parts, *refs):
    outs = refs[:-1]
    quarter = parts[0].shape[1] // (TAPS * len(outs))
    for k in range(4):
        ref = parts[k]
        there = pl.ds(pl.multiple_of(tasks[k] * quarter, quarter), quarter)
        for layer, out in enumerate(outs):
            for t in range(TAPS):
                start = (layer * TAPS + t) * quarter
                out[t, :, there] = ref[:, start : start + quarter].astype(F32)


def branch_result_kernel(
    tasks, norm_tasks, parts, norms, features, out, in_out, mask_out, gains, biases, pools, fv, sems
):
    io = Copies(sems)
    read = io.start(features.at[pl.ds(0, TASKS)], fv)
    channels = in_out.shape[2]
    for k in range(4):
        ref = parts[k]
        task = tasks[k]

        @pl.when(task < TASKS)
        def _():
            for t in range(TAPS + 2):
                block = ref[:, t * channels : (t + 1) * channels].astype(F32)
                if t < TAPS:
                    out[task, t] = block
                elif t == TAPS:
                    in_out[task] = block
                else:
                    mask_out[task] = block

        @pl.when(norm_tasks[k] < TASKS)
        def _():
            gains[norm_tasks[k]] = norms[k][0:3, :]
            biases[norm_tasks[k]] = norms[k][3:6, :]

    read.wait()
    io.put(fv, pools)
    io.finish()


VMEM = pl.BlockSpec(memory_space=pltpu.VMEM)
VMEM_LIMIT = 28 * MIB


class Near:
    def __init__(self, value):
        self.value = value


class Far(Near):
    pass


class Free:
    def __init__(self, value):
        self.value = value


def frees(values):
    return [Free(value) for value in values]


def nears(values):
    return [Near(value) for value in values]


def bytes_of(a):
    return math.prod(a.shape) * jnp.dtype(a.dtype).itemsize


def run(kernel, ins, outs, scratch, flops=0, copies=64, near=False, deps=(), aliases=None):
    flat, specs, groups = [], [], []
    for item in ins:
        parts = list(item) if isinstance(item, (list, tuple)) else [item]
        groups.append(len(parts) if isinstance(item, (list, tuple)) else 0)
        for part in parts:
            kept, free = near or isinstance(part, Near), isinstance(part, Free)
            kept = kept and not isinstance(part, Far)
            part = part.value if isinstance(part, (Near, Free)) else part
            if part.ndim == 1:
                specs.append(SMEM)
                part = pltpu.with_memory_space_constraint(part, pltpu.HBM)
            elif free:
                specs.append(ANY)
            elif kept:
                specs.append(VMEM)
                if not near:
                    part = pltpu.with_memory_space_constraint(part, pltpu.VMEM)
            else:
                specs.append(HBM)
                part = pltpu.with_memory_space_constraint(part, pltpu.HBM)
            flat.append(part)
    shapes, out_specs = [], []
    for item in outs:
        kept = (near or isinstance(item, Near)) and not isinstance(item, Far)
        item = item.value if isinstance(item, Near) else item
        if not near:
            item = (pltpu.VMEM if kept else pltpu.HBM)(item.shape, item.dtype)
        shapes.append(item)
        out_specs.append(VMEM if kept else HBM)
    size = sum(bytes_of(a) for a in flat) + sum(bytes_of(o) for o in shapes)
    count = len(flat)

    def body(*refs):
        rest, args = list(refs[:count]), []
        for group in groups:
            if group:
                args.append(tuple(rest[:group]))
                rest = rest[group:]
            else:
                args.append(rest.pop(0))
        kernel(*args, *refs[count + len(deps) :])

    return pl.pallas_call(
        body,
        out_shape=shapes,
        in_specs=specs + [ANY if isinstance(d, Free) else HBM for d in deps],
        out_specs=out_specs,
        scratch_shapes=list(scratch) + [pltpu.SemaphoreType.DMA((copies,))],
        input_output_aliases=aliases or {},
        compiler_params=pltpu.CompilerParams(vmem_limit_bytes=VMEM_LIMIT),
        cost_estimate=pl.CostEstimate(flops=flops, bytes_accessed=size, transcendentals=0),
    )(*flat, *(d.value if isinstance(d, Free) else pltpu.with_memory_space_constraint(d, pltpu.HBM) for d in deps))


def after(value, *others):
    return pl.pallas_call(
        lambda *refs: None,
        out_shape=jax.ShapeDtypeStruct(value.shape, value.dtype),
        in_specs=[HBM] + [ANY] * len(others),
        out_specs=HBM,
        input_output_aliases={0: 0},
    )(value, *others)


def swap(value, axis, mask):
    pairs = [(i, i ^ mask) for i in range(lax.axis_size(axis))]
    return lax.ppermute(value, axis, pairs)


def cross(value, second):
    tasks, width = lax.axis_size("task"), lax.axis_size("dp")
    pairs = []
    for t in range(tasks):
        for d in range(width):
            mask = 1 if (d + second) % 2 == 0 else 2
            pairs.append((t * width + d, (t ^ mask) * width + d))
    return lax.ppermute(value, ("task", "dp"), pairs)


def all_of(value, axis, unit):
    if lax.axis_size(axis) == 4 * unit:
        return [value] + [swap(value, axis, unit * k) for k in (1, 2, 3)]
    mask = unit
    while mask < lax.axis_size(axis):
        value = value + swap(value, axis, mask)
        mask *= 2
    return [value]


def total(parts):
    return (parts[0] + parts[1]) + (parts[2] + parts[3]) if len(parts) == 4 else parts[0]


def sum_parts(pay):
    return all_of(pay + swap(pay, "dp", 1), "dp", 2)


def exchange(pay):
    recv = swap(pay, "dp", 1)
    return recv, all_of(pay[COLS:] + recv[COLS:], "dp", 2)


def join(*parts):
    return jnp.concatenate(parts, axis=0)


def gather_column(part, *others):
    far = swap(part, "dp", 6)
    return join(part, swap(part, "dp", 2), swap(part, "dp", 4), after(far, *others) if others else far)


def plane(part, *others):
    first, second = cross(part, 0), cross(part, 1)
    return [part, first, second, cross(after(first, *others) if others else first, 1)]


def gather_core(parts):
    return parts + [swap(part, "dp", 1) for part in parts]


def domain_counts(size_class, domain_tags):
    big_area = HEIGHT * WIDTH
    small_area = BAND * HALF_WIDTH
    ones_count = jnp.sum(
        jnp.where(
            size_class == 0, big_area * domain_tags[:, 0], small_area * jnp.sum(domain_tags, axis=1)
        )
    )
    all_count = size_class.shape[0] * big_area
    return jnp.maximum(jnp.stack([all_count - ones_count, ones_count]).astype(F32), 1.0)


def on_device(
    images,
    conv_first,
    conv_second,
    conv_third,
    trunk_gains,
    trunk_biases,
    attend_in,
    attend_mask,
    attend_out,
    branch_gains,
    branch_biases,
    size_class,
    domain_tags,
    trunk_cotangent,
    task_cotangent,
):
    rows, cols, ch = images.shape
    pixels = rows * cols
    position = lax.axis_index("dp")
    task_index = lax.axis_index("task")
    width = lax.axis_size("dp")
    task_count = lax.axis_size("task")
    quarter = ch // task_count
    own_out = ch // width
    by_permute = width == 8 and task_count == 4 and own_out == task_count * PIECE
    pair_index = position // 2
    bottom = position % 2
    local_class = lax.dynamic_slice_in_dim(size_class, pair_index * CANVAS, CANVAS, 0)
    local_tags = lax.dynamic_slice_in_dim(domain_tags, pair_index * CANVAS, CANVAS, 0)
    side = jnp.arange(GROUPS) % 2
    slot_class = jnp.repeat(local_class, 2)
    slot_tags = jnp.repeat(local_tags, 2, axis=0)
    which = jnp.where(slot_class == 1, bottom * 2 + side, 0)
    groups = jnp.sum(slot_tags * (jnp.arange(4)[None, :] == which[:, None]), axis=1)
    active = (task_index < TASKS).astype(jnp.int32)
    branch = jnp.minimum(task_index, TASKS - 1)
    info = jnp.concatenate(
        [groups, local_class, jnp.stack([bottom, task_index, active, branch, position])]
    ).astype(jnp.int32)
    cnt = domain_counts(size_class, domain_tags)

    def shape(dims, dtype=F32):
        return jax.ShapeDtypeStruct(dims, dtype)

    z_index, core = position // 2, position % 2
    masks_of = (jnp.where(core == 0, 1, 2), jnp.where(core == 0, 2, 1))
    places = []
    for side_core, (m1, m2) in ((core, masks_of), (1 - core, masks_of[::-1])):
        for t in (task_index, task_index ^ m1, task_index ^ m2, task_index ^ m1 ^ m2):
            for zz in (z_index, z_index ^ 1, z_index ^ 2, z_index ^ 3):
                places.append((2 * zz + side_core) * own_out + t * (own_out // task_count))
    place = jnp.stack(places).astype(jnp.int32)
    pieces_of_task = [task_index, task_index ^ masks_of[0], task_index ^ masks_of[1], task_index ^ 3]
    task_order = jnp.stack(pieces_of_task).astype(jnp.int32)
    norm_order = jnp.stack([task_index ^ k for k in range(4)]).astype(jnp.int32)
    spot = jnp.stack([task_index, branch]).astype(jnp.int32)

    def by_tap(kernel):
        kernel = jnp.swapaxes(kernel, -1, -2)
        tasks = kernel.shape[:1] if kernel.ndim % 2 else ()
        return kernel.reshape(tasks + (-1,) + kernel.shape[-2:])

    def cast(sources, out_rows, pick, deps=()):
        sources = [by_tap(k) for k in sources]
        taps_of = [k.shape[-3] for k in sources]
        (out,) = pl.pallas_call(
            functools.partial(cast_kernel, pick, len(sources)),
            out_shape=[shape((out_rows, sum(taps_of) * ch), BF)],
            in_specs=[SMEM] + [HBM] * len(sources) + [ANY] * len(deps),
            out_specs=[VMEM],
            scratch_shapes=[pltpu.VMEM((n, out_rows, ch), F32) for n in taps_of]
            + [pltpu.SemaphoreType.DMA((len(sources),))],
            compiler_params=pltpu.CompilerParams(vmem_limit_bytes=VMEM_LIMIT),
        )(spot, *(pltpu.with_memory_space_constraint(k, pltpu.HBM) for k in sources), *deps)
        return out

    def pick(values):
        return lax.dynamic_index_in_dim(values, branch, 0, keepdims=False)

    params = jnp.concatenate(
        [trunk_gains, pick(branch_gains), trunk_biases, pick(branch_biases), jnp.zeros((4, ch), F32)]
    )
    flat = images.reshape(pixels, ch)
    edge = jnp.where(bottom == 1, flat[:COLS], flat[pixels - COLS :])
    gather = functools.partial(lax.all_gather, axis_name="dp", axis=0, tiled=True)
    halo = swap(edge, "dp", 1)
    cast_pair = cast([attend_in, attend_mask], own_out, False)
    cast_out = cast([attend_out], own_out, False)
    early = [Free(halo)]
    if by_permute:
        casts = [cast([conv_third], PIECE, True), cast_pair, cast_out, halo]
        column_1 = gather_column(cast([conv_first], PIECE, True), *casts)
        first, second = cross(column_1, 0), cross(column_1, 1)
        plane_1 = [column_1, first, second, cross(after(first, second), 1)]
        weights_1 = gather_core(plane_1)
        weights_2 = [gather(after(cast([conv_second], own_out, False), column_1))]
    else:
        weights_1, weights_2, weights_3 = [
            [gather(cast([k], own_out, False))] for k in (conv_first, conv_second, conv_third)
        ]
    weights = [weights_1, weights_2, None]
    w_pair = gather(cast_pair)
    w_out = gather(cast_out)

    wide = shape((pixels, ch))
    low_wide = shape((pixels, ch), BF)
    pay_shape = shape((COLS + 8, ch))
    sums_shape = shape((8, ch))
    taps_dims = (3, pixels + 2 * COLS, ch)
    v_wide = pltpu.VMEM((pixels, ch), F32)
    v_pay = pltpu.VMEM((COLS + 8, ch), F32)
    v_low = pltpu.VMEM((pixels, ch), BF)
    v_sums = pltpu.VMEM((8, ch), F32)
    v_pool = pltpu.VMEM((pixels // 4, ch), BF)
    v_conv = pltpu.VMEM((ch, TAPS * ch), BF)
    v_dot = pltpu.VMEM((ch, ch), BF)
    v_quarter = pltpu.VMEM((3, pixels + 2 * COLS, quarter), BF)
    taps = pltpu.VMEM(taps_dims, BF)
    masks = pltpu.VMEM((2, COLS, 128), F32)
    acc = pltpu.VMEM((2, GROUPS, 8, ch), F32)
    buf = pltpu.VMEM((ch // 128, COLS, 128), F32)

    def coefs(blocks):
        return pltpu.VMEM((4 * blocks, ch), F32)

    conv_flops = 2 * TAPS * pixels * ch * ch
    dot_flops = 2 * pixels * ch * ch

    quarter_shape = shape((3, pixels + 2 * COLS, quarter), BF)
    z, recv, stats, quarters = [], [], [], []
    outs = [wide, Near(wide), Near(pay_shape), quarter_shape]
    near = None
    kept = []
    for layer in range(3):
        if layer == 0:
            values, near, pay, part = run(
                functools.partial(first_conv_kernel, rows),
                [info, place, flat, Near(halo), weights_1],
                outs, [v_low, v_conv, taps, masks, acc], conv_flops, deps=early,
            )
            if by_permute:
                column_3 = gather_column(after(casts[0], weights_1[4]), pay)
                first, second = cross(column_3, 0), cross(column_3, 1)
        else:
            values, near, pay, part, held = run(
                functools.partial(conv_kernel, rows, layer - 1),
                [info, cnt, place, Near(params), Near(near) if layer == 2 else z[-1], Near(recv[-1]), nears(stats[-1]), weights[layer]],
                outs + [sums_shape],
                ([] if layer == 2 else [v_wide]) + [v_sums, v_conv, taps, masks, acc, coefs(4)], conv_flops,
            )
            kept.append(held)
            if layer == 1:
                if by_permute:
                    plane_3 = [column_3, first, second, cross(after(first, second, pay), 1)]
                    weights[2] = gather_core(plane_3)
                else:
                    weights[2] = weights_3
        got, found = exchange(pay)
        z.append(values)
        recv.append(got)
        stats.append(found)
        quarters.append(part)

    low, trunk_pool, u, near, pay, held = run(
        functools.partial(enter_kernel, rows, 2),
        [info, cnt, Near(params), z[2], Near(recv[2]), nears(stats[2]), w_pair],
        [shape((pixels + COLS, ch), BF), shape((pixels // 4, ch), BF), wide, Near(wide), Near(sums_shape),
         sums_shape],
        [v_wide, v_sums, v_dot, pltpu.VMEM((pixels + COLS, ch), BF), v_pool, acc,
         coefs(4), buf], dot_flops,
    )
    kept.append(held)
    u_stats = sum_parts(pay)
    p, q, near, pay, u_kept = run(
        functools.partial(mask_kernel, rows, 3),
        [info, cnt, Near(params), Near(near), nears(u_stats), w_pair],
        [low_wide, wide, Near(wide), Near(pay_shape), sums_shape],
        [v_sums, v_dot, v_low, acc, coefs(4)], dot_flops,
    )
    q_recv, q_stats = exchange(pay)
    y, near, pay, masked_taps, q_kept = run(
        functools.partial(branch_conv_kernel, rows, 4),
        [info, cnt, Near(params), low, q, Near(q_recv), nears(q_stats), w_out],
        [wide, Near(wide), Near(pay_shape), shape(taps_dims, BF), sums_shape],
        [v_wide, pltpu.VMEM((pixels + COLS, ch), BF), v_sums, v_conv, taps, masks, acc, coefs(4)], conv_flops,
    )
    y_recv, y_stats = exchange(pay)

    branch_pool, near, pay, y_kept = run(
        functools.partial(turn_kernel, rows, 5),
        [info, cnt, Near(params), Near(near), nears(y_stats), task_cotangent.reshape(TASKS, pixels // 4, ch)],
        [shape((pixels // 4, ch), BF), wide, Near(pay_shape), sums_shape],
        [v_wide, v_sums, v_pool, v_pool, acc, coefs(4), buf],
    )
    task_features = lax.all_gather(branch_pool, "task")
    gy_recv, y_sums = exchange(pay)
    e_y, near, gs, pay, norms = run(
        functools.partial(branch_back_kernel, rows),
        [info, cnt, Near(params), near, y, Near(gy_recv), y_recv, y_kept, nears(y_sums), w_out, low, q,
         q_kept],
        [low_wide, Near(wide), wide, Near(sums_shape), Near(sums_shape)],
        [v_wide, v_wide, v_pay, v_sums, v_sums, v_sums, v_low, v_wide, v_low, v_conv,
         taps, masks, acc, coefs(10)], conv_flops,
    )
    q_sums = sum_parts(pay)
    e_q, near, pay, norms = run(
        functools.partial(mask_back_kernel, rows),
        [info, cnt, Near(params), Near(near), q, q_kept, nears(q_sums), w_pair, u, u_kept, Near(norms)],
        [low_wide, Near(wide), Near(sums_shape), Near(sums_shape)],
        [v_wide, v_wide, v_sums, v_sums, v_sums, v_dot, v_low, acc, coefs(10)], dot_flops,
    )
    u_sums = sum_parts(pay)
    e_u, grad_shared, pay, norms = run(
        functools.partial(leave_kernel, rows),
        [info, cnt, Near(params), Near(near), u, u_kept, nears(u_sums), w_pair, gs, z[2], kept[2],
         trunk_cotangent.reshape(pixels // 4, ch), Near(norms)],
        [low_wide, low_wide, Near(sums_shape), Near(sums_shape)],
        [v_wide, v_wide, v_sums, v_sums, v_sums, v_dot, v_wide, v_wide, v_pool, v_low, v_low, acc,
         coefs(10), buf], dot_flops,
    )
    sums = all_of(total(sum_parts(pay)), "task", 1)
    norm_parts = [norms] + [swap(norms, "task", k) for k in (1, 2, 3)]
    grad_half = grad_shared + after(cross(grad_shared, 0), *sums, *norm_parts, task_features)
    grad_rest = cross(grad_half, 1)
    (branch_part,) = run(
        functools.partial(branch_wgrad_kernel, rows),
        [masked_taps, e_y, p, e_q, low, e_u],
        [shape((ch, 11 * ch), BF)],
        [taps, v_low, v_low, v_low, v_low, v_low, pltpu.VMEM((ch, 11 * ch), BF)], conv_flops, deps=[grad_half],
    )
    branch_part = after(branch_part, grad_rest)
    branch_part = lax.psum_scatter(branch_part, "dp", scatter_dimension=0, tiled=True)

    edge = jnp.where(
        bottom == 1, grad_half[:COLS] + grad_rest[:COLS], grad_half[-COLS:] + grad_rest[-COLS:]
    )
    g, g_recv = [grad_half, grad_rest], swap(edge, "dp", 1)
    trunk_norms = jnp.zeros((8, ch), F32)
    for layer in (2, 1):
        top = layer == 2
        e, near, pay, trunk_norms = run(
            functools.partial(trunk_back_kernel, rows, layer, top),
            [info, cnt, place, Near(params), g, z[layer], Near(g_recv), recv[layer], kept[layer], nears(sums),
             z[layer - 1], kept[layer - 1], Near(trunk_norms), weights[layer]],
            [low_wide, wide, Near(pay_shape), Near(sums_shape)],
            [v_wide, v_wide, v_pay, v_sums, v_sums, v_wide, v_sums, v_low, v_conv, taps, masks, coefs(10), acc] + ([v_low, v_low] if top else [v_wide]), conv_flops,
            deps=() if top else [trunk_part],
        )
        g_recv, sums = exchange(pay)
        g = [near]
        (trunk_part,) = run(
            functools.partial(trunk_wgrad_kernel, rows, layer - 1),
            [quarters[layer], e] + ([] if top else [trunk_part]), [shape((ch, 2 * TAPS * quarter), BF)],
            [v_quarter, v_low, pltpu.VMEM((ch, TAPS * quarter), BF)], conv_flops // 4,
            deps=() if top else frees(sums[:2]), aliases=None if top else {2: 0},
        )

    later_part = lax.psum_scatter(trunk_part, "dp", scatter_dimension=0, tiled=True)
    half_out = shape((ch // 2, TAPS * quarter), BF)
    last_kernel = functools.partial(last_grad_kernel, rows)
    if not by_permute:
        last_kernel = functools.partial(whole_last_grad_kernel, rows)
    e, trunk_gains_grad, trunk_biases_grad, *halves = run(
        last_kernel,
        [info, place, cnt, Near(params), g[0], z[0], Near(g_recv), recv[0], kept[0], nears(sums), quarters[0],
         Near(trunk_norms)],
        [shape((pixels + 2 * COLS, ch), BF), Near(shape((3, ch))), Near(shape((3, ch)))]
        + ([half_out, half_out] if by_permute else [shape((ch, TAPS * quarter), BF)]),
        [v_wide, v_wide, v_pay, v_sums, v_sums, v_quarter, pltpu.VMEM((pixels + 2 * COLS, ch), BF),
         pltpu.VMEM((ch, TAPS * quarter), BF), coefs(10)], conv_flops // 4, deps=[trunk_part],
    )

    high = rows // 2
    tile = high * COLS

    def input_grad(m, before, deps):
        ins = [info, place, e, weights[0]] + before
        (out,) = run(
            functools.partial(last_conv_kernel, m, high), ins, [wide],
            [pltpu.VMEM((tile + 2 * COLS, ch), BF), pltpu.VMEM((tile, ch), F32), v_conv,
             pltpu.VMEM((3, tile + 2 * COLS, ch), BF), masks], conv_flops // 2, deps=deps,
            aliases={3 + len(weights[0]): 0} if before else None,
        )
        return [out]

    if by_permute:
        mine, other = halves
        half = mine.shape[0] // 2
        got = swap(other, "dp", 1)
        branch_part = after(branch_part, got)
        branch_first, branch_second = cross(branch_part, 0), cross(branch_part, 1)
        images_grad = input_grad(0, [], [Free(got)])
        send, keep = mine[half:] + got[half:], mine[:half] + got[:half]
        got = after(swap(send, "dp", 2), images_grad[0], branch_first, branch_second)
        images_grad = input_grad(1, images_grad, [Free(got)])
        branch_third = cross(branch_first, 1)
        half = half // 2
        send, keep = keep[half:] + got[half:], keep[:half] + got[:half]
        got = after(swap(send, "dp", 4), images_grad[0], branch_third)
        first_part = keep + got
        trunk_parts = plane(jnp.concatenate([first_part, later_part], axis=1))
        branch_parts = [branch_part, branch_first, branch_second, branch_third]
        result_deps = [Free(trunk_parts[1])]
    else:
        first_part = lax.psum_scatter(halves[0], "dp", scatter_dimension=0, tiled=True)
        images_grad, result_deps = [], []
        for m in range(2):
            images_grad = input_grad(m, images_grad, [])
        trunk_parts = plane(jnp.concatenate([first_part, later_part], axis=1))
        branch_parts = plane(branch_part)
    images_grad = images_grad[0]
    out_grad, in_grad, mask_grad, branch_gains_grad, branch_biases_grad, pools = run(
        branch_result_kernel,
        [task_order, norm_order, branch_parts, norm_parts,
         Far(task_features)],
        [shape((TASKS, TAPS, own_out, ch)), shape((TASKS, own_out, ch)), shape((TASKS, own_out, ch)),
         shape((TASKS, 3, ch)), shape((TASKS, 3, ch)), Far(shape((TASKS, pixels // 4, ch), BF))],
        [pltpu.VMEM((TASKS, pixels // 4, ch), BF)], near=True, deps=result_deps,
    )
    grad_shape = shape((TAPS, own_out, ch))
    grads = run(trunk_result_kernel, [task_order, trunk_parts], [grad_shape] * 3, [], near=True)
    kernel_grads = [
        jnp.swapaxes(k.reshape(3, 3, own_out, ch), 2, 3) for k in grads
    ]
    return (
        trunk_pool.reshape(rows // 2, cols // 2, ch),
        pools.reshape(TASKS, rows // 2, cols // 2, ch),
        images_grad.reshape(rows, cols, ch),
        *kernel_grads,
        trunk_gains_grad,
        trunk_biases_grad,
        jnp.swapaxes(in_grad, 1, 2),
        jnp.swapaxes(mask_grad, 1, 2),
        jnp.swapaxes(out_grad.reshape(TASKS, 3, 3, own_out, ch), 3, 4),
        branch_gains_grad,
        branch_biases_grad,
    )


def solution(mesh):
    in_specs = (
        P("dp", None, None),
        P(None, None, None, "dp"),
        P(None, None, None, "dp"),
        P(None, None, None, "dp"),
        P(),
        P(),
        P(None, None, "dp"),
        P(None, None, "dp"),
        P(None, None, None, None, "dp"),
        P(),
        P(),
        P(),
        P(),
        P("dp", None, None),
        P(None, "dp", None, None),
    )
    out_specs = (
        P("dp", None, None),
        P(None, "dp", None, None),
        P("dp", None, None),
        P(None, None, None, "dp"),
        P(None, None, None, "dp"),
        P(None, None, None, "dp"),
        P(),
        P(),
        P(None, None, "dp"),
        P(None, None, "dp"),
        P(None, None, None, None, "dp"),
        P(),
        P(),
    )
    return jax.shard_map(
        on_device, mesh=mesh, in_specs=in_specs, out_specs=out_specs, check_vma=False
    )
```
